512 devices in a mesh: expert: 128 (over y, z, core), dp: 4 (over x).
Axes of the slice: x: 4, y: 8, z: 8, core: 2. Of those that a mesh axis runs over, the one named last changes fastest.
Arguments:
- tokens: bfloat16 [4096, 2048], P('expert', 'dp'), may hold values from -6 to 6
- out_grad: bfloat16 [4096, 2048], P('expert', 'dp'), may hold values from -6 to 6
- routes: int32 [4096, 8], P('expert'), may hold values from 0 to 127, all different within a row; in each aligned block of 32 rows (0 to 31, 32 to 63, ...) at most 2 rows name the same one
- route_weight: float32 [4096, 8], P('expert'), may hold values from 0.05 to 0.5
- placement: int32 [128], replicated, may hold values from 0 to 127, each once
- gate_weight: bfloat16 [128, 2048, 768], P('expert', 'dp'), may hold values from -0.125 to 0.125
- up_weight: bfloat16 [128, 2048, 768], P('expert', 'dp'), may hold values from -0.125 to 0.125
- down_weight: bfloat16 [128, 768, 2048], P('expert', None, 'dp'), may hold values from -0.21875 to 0.21875
Outputs:
- in_grad: bfloat16 [4096, 2048], P('expert', 'dp')
- gate_grad: bfloat16 [128, 2048, 768], P('expert', 'dp')
- up_grad: bfloat16 [128, 2048, 768], P('expert', 'dp')
- down_grad: bfloat16 [128, 768, 2048], P('expert', None, 'dp')
The draws below stay inside these ranges and needn't reach their ends.
Inputs may be any that keep to these rules, and one draw needn't show every extreme that they name: `routes`: each row names 8 different experts. In each aligned block of 32 rows (the tokens of one index of the expert axis) no expert is named by more than 2 rows, a bound that some block reaches. `placement`: each index appears once.
All inputs are finite; a program needn't handle non-finite values.
Results may differ from the reference program's by a relative error of at most 0.025.
Values may be sent and summed in bfloat16 or wider, within the bound.
A program may use at most 64 MiB of HBM per device.

```python
import math
import jax
import jax.numpy as jnp
import numpy as np
from jax import lax

D = 2048
F = 768
TOP = 8
TOK_DEV = 32
EXPERTS = 128
CAP = 2
TOKENS = 4096
N_EXPERT = 128
N_DP = 4


def levels(stream_key, shape, cuts, smallest, high):
    gain, own = 1.0, jax.random.fold_in(stream_key, 6)
    for axis_at, parts in cuts:
        heights = jnp.exp(jax.random.uniform(jax.random.fold_in(own, axis_at), (parts,), jnp.float32, smallest / len(cuts), high / len(cuts)))
        gain = gain * jnp.repeat(heights, shape[axis_at] // parts).reshape([-1 if axis == axis_at else 1 for axis in range(len(shape))])
    return gain


def deal_out(rng, own, number, rows, amount, top, limit, skew):
    order = jax.random.permutation(rng, amount)
    packed, common = shares(amount, rows * top, limit, skew, True), shares(amount, rows * top, limit, skew, False)
    places = jnp.arange(amount)

    def named(tallies, offset_by):
        used = int((tallies > 0).sum())
        fixed = max(1, used // 4)
        moved = fixed + (places - fixed + offset_by * (used - fixed)) % max(1, amount - fixed)
        return jnp.zeros((amount,), jnp.int32).at[order[jnp.where(places < fixed, places, moved)]].set(jnp.asarray(tallies, jnp.int32))

    tallies = jnp.where(number % 4 == 0, named(packed, number // 4), named(common, number - number // 4 - 1))
    mixed = jax.random.permutation(jax.random.fold_in(own, 3), amount)
    donor, receiver = mixed[0:amount // 2 * 2:2], mixed[1:amount // 2 * 2:2]
    margin = jnp.minimum(tallies[donor] - 1, limit - tallies[receiver]) // 2
    margin = jnp.where((donor == order[0]) | (receiver == order[0]) | (tallies[receiver] == 0), 0, jnp.maximum(margin, 0))
    moved = jax.random.randint(jax.random.fold_in(own, 4), (amount // 2,), 0, 1 << 20) % (margin + 1)
    tallies = tallies.at[donor].add(-moved).at[receiver].add(moved)
    items = jnp.searchsorted(jnp.cumsum(tallies), jnp.arange(rows * top), side="right").astype(jnp.int32)
    table = items.reshape(top, rows).T
    table = table[jax.random.permutation(jax.random.fold_in(own, 1), rows)]
    offset_by = jax.random.randint(jax.random.fold_in(own, 2), (rows, 1), 0, top)
    return jnp.take_along_axis(table, (jnp.arange(top)[None, :] + offset_by) % top, axis=1)


def shares(count, total, limit, lean, full):
    loads = [(1 << 20) // math.isqrt(grade ** lean) + 1 for grade in range(1, count + 1)]
    largest = limit if full else min(limit, max(-(-total // count), total * loads[0] // sum(loads)))
    least = 1 if total - largest >= count - 1 else 0
    given, spare = [largest] + [least] * (count - 1), total - largest - least * (count - 1)
    while spare > 0:
        free = [i for i in range(1, count) if given[i] < largest] or [i for i in range(1, count) if given[i] < limit]
        pool, budget = sum([loads[i] for i in free]), spare
        for i in free:
            more = min(limit - given[i], max(1, budget * loads[i] // pool), spare)
            given[i] = given[i] + more
            spare = spare - more
    return np.array(given)


def gaussian(key, dims, spread, bound, shards=(), kind=jnp.bfloat16):
    values = spread * jax.random.normal(key, dims, jnp.float32)
    if shards:
        values = values * levels(key, dims, shards, -0.22, 0.18)
    return jnp.clip(values, -bound, bound).astype(kind)


def setup_inputs(seed: int = 0) -> dict:
    key_list = jax.random.split(jax.random.key(seed), 9)
    tokens = gaussian(key_list[0], (TOKENS, D), 1.0, 6.0, ((0, 128), (1, 4)))
    out_grad = gaussian(key_list[1], (TOKENS, D), 1.0, 6.0, ((0, 128), (1, 4)))
    routes_keys = jax.random.split(jax.random.fold_in(key_list[2], 1), TOKENS // TOK_DEV)
    routes_turns = jax.random.permutation(jax.random.fold_in(key_list[2], 3), TOKENS // TOK_DEV)
    routes = jax.vmap(lambda own, number: deal_out(jax.random.fold_in(key_list[2], 2), own, number, TOK_DEV, EXPERTS, TOP, CAP, 2))(routes_keys, routes_turns).reshape((TOKENS, TOP))
    route_weight = jnp.clip(jnp.exp(math.log(0.5) - 2.3025851 * jax.random.uniform(key_list[3], (TOKENS, TOP), jnp.float32) ** levels(key_list[3], (TOKENS, TOP), ((0, 128),), -0.2, 0.2)), 0.05, 0.5)
    placement = jax.random.permutation(key_list[4], EXPERTS).astype(jnp.int32)
    gate_weight = gaussian(key_list[5], (EXPERTS, D, F), D ** -0.5, 0.125, ((0, 128), (1, 4)))
    up_weight = gaussian(key_list[6], (EXPERTS, D, F), D ** -0.5, 0.125, ((0, 128), (1, 4)))
    down_weight = gaussian(key_list[7], (EXPERTS, F, D), F ** -0.5, 0.21875, ((0, 128), (2, 4)))
    return {"tokens": tokens, "out_grad": out_grad, "routes": routes, "route_weight": route_weight, "placement": placement, "gate_weight": gate_weight, "up_weight": up_weight, "down_weight": down_weight}


def blocked_sum(left, right):
    slots = left.shape[0]
    part = left.shape[1] // N_DP
    pieces = jnp.einsum("sbd,bdf->bsf", left.reshape(slots, N_DP, part), right.reshape(N_DP, part, right.shape[1]), precision=lax.Precision.HIGHEST)
    pieces = lax.optimization_barrier(pieces.astype(jnp.bfloat16)).astype(jnp.float32)
    return jnp.sum(pieces, axis=0)


def reference(tokens, out_grad, routes, route_weight, placement, gate_weight, up_weight, down_weight):
    chosen = routes.shape[1]
    slots = N_EXPERT * CAP
    flat_expert = routes.reshape(-1)
    flat_weight = route_weight.reshape(-1).astype(jnp.float32)
    host_ids = jnp.arange(placement.shape[0], dtype=jnp.int32)
    high = lax.Precision.HIGHEST

    def per_host(carry, inputs):
        host, gate_one, up_one, down_one = inputs
        expert = jnp.sum(jnp.where(placement == host, host_ids, 0)).astype(jnp.int32)
        picked = flat_expert == expert
        found = jnp.nonzero(picked, size=slots, fill_value=0)[0].astype(jnp.int32)
        valid = (jnp.arange(slots, dtype=jnp.int32) < jnp.sum(picked.astype(jnp.int32))).astype(jnp.float32)[:, None]
        token_row = (found // chosen).astype(jnp.int32)
        rows = tokens[token_row].astype(jnp.float32) * valid
        scaled = (flat_weight[found][:, None] * out_grad[token_row].astype(jnp.float32)).astype(jnp.bfloat16)
        scaled = lax.optimization_barrier(scaled).astype(jnp.float32) * valid
        gate_f = gate_one.astype(jnp.float32)
        up_f = up_one.astype(jnp.float32)
        down_f = down_one.astype(jnp.float32)
        gate_sum = blocked_sum(rows, gate_f)
        up_sum = blocked_sum(rows, up_f)
        hidden_grad = blocked_sum(scaled, down_f.T)
        sigma = jax.nn.sigmoid(gate_sum)
        active = gate_sum * sigma
        hidden = lax.optimization_barrier((active * up_sum).astype(jnp.bfloat16)).astype(jnp.float32)
        gate_back = (hidden_grad * up_sum * sigma * (1.0 + gate_sum * (1.0 - sigma))).astype(jnp.bfloat16)
        up_back = (hidden_grad * active).astype(jnp.bfloat16)
        gate_back = lax.optimization_barrier(gate_back).astype(jnp.float32)
        up_back = lax.optimization_barrier(up_back).astype(jnp.float32)
        row_back = jnp.dot(gate_back, gate_f.T, precision=high) + jnp.dot(up_back, up_f.T, precision=high)
        row_back = lax.optimization_barrier(row_back.astype(jnp.bfloat16)).astype(jnp.float32)
        carry = carry.at[token_row].add(row_back)
        gate_grad = jnp.dot(rows.T, gate_back, precision=high).astype(jnp.bfloat16)
        up_grad = jnp.dot(rows.T, up_back, precision=high).astype(jnp.bfloat16)
        down_grad = jnp.dot(hidden.T, scaled, precision=high).astype(jnp.bfloat16)
        return carry, (gate_grad, up_grad, down_grad)

    start = jnp.zeros(tokens.shape, jnp.float32)
    total, grads = lax.scan(per_host, start, (host_ids, gate_weight, up_weight, down_weight))
    return total.astype(jnp.bfloat16), grads[0], grads[1], grads[2]
```

```python
import functools

import jax
import jax.numpy as jnp
from jax import lax
from jax.experimental import pallas as pl
from jax.experimental.pallas import tpu as pltpu
from jax.sharding import PartitionSpec as P

BF = jnp.bfloat16
F32 = jnp.float32
LANES = 128


def matmul(left, right, left_dim=1, right_dim=0):
    return lax.dot_general(
        left, right, (((left_dim,), (right_dim,)), ((), ())), preferred_element_type=F32
    )


def remote(src, dst, send_sem, recv_sem, device):
    return pltpu.make_async_remote_copy(
        src_ref=src,
        dst_ref=dst,
        send_sem=send_sem,
        recv_sem=recv_sem,
        device_id=device,
        device_id_type=pl.DeviceIdType.MESH,
    )


def kernel(
    side, parts,
    tokens, out_grad, routes, route_weight, placement, gate_hbm, up_hbm, down_hbm,
    in_grad, gate_grad_hbm, up_grad_hbm, down_grad_hbm,
    gate, up, down, gate_grad, up_grad, down_grad,
    send0, send1, mid0, mid1, recv, rows_all, grad_all,
    psend, precv, full, ret, rmid, fin0, fin1, spread, select,
    load_sem, store_sem, s1_send, s1_recv, s2_send, s2_recv,
    p_send, p_recv, a_send, a_recv, r1_send, r1_recv, r2_send, r2_recv,
):
    n = side
    experts = 2 * n * n
    count_tok, width = tokens.shape
    chunks = width // LANES
    units = 2 * chunks
    hidden_dim = gate.shape[1]
    chosen = routes.shape[1]
    span = experts // parts
    me = lax.axis_index("expert")
    d = lax.axis_index("dp")
    y = me // (2 * n)
    z = lax.rem(me // 2, n)
    c = lax.rem(me, 2)

    def at(yy, zz, cc):
        return {"expert": (yy * n + zz) * 2 + cc}

    def turn(base, i):
        return lax.rem(base + i, n)

    loads = [
        pltpu.make_async_copy(src.at[0], dst, load_sem.at[i])
        for i, (src, dst) in enumerate(((gate_hbm, gate), (up_hbm, up), (down_hbm, down)))
    ]
    for load in loads:
        load.start()

    barrier = pltpu.get_barrier_semaphore()
    greeted = [at(y, z, 1 - c)]
    for i in range(1, n):
        for cc in range(2):
            greeted += [at(turn(y, i), z, cc), at(y, turn(z, i), cc)]
    greeted += [{"dp": lax.rem(d + i, parts)} for i in range(1, parts)]
    for device in greeted:
        pl.semaphore_signal(
            barrier, inc=1, device_id=device, device_id_type=pl.DeviceIdType.MESH
        )

    place = placement[...]
    place_y, place_z, place_c = place // (2 * n), lax.rem(place // 2, n), lax.rem(place, 2)
    spot = jnp.where(place_c == 0, place_y * n + place_z, n * n + place_z * n + place_y)
    spot = spot.astype(F32)
    expert_ids = lax.broadcasted_iota(jnp.int32, (count_tok, experts), 1)
    expert_ids_f = expert_ids.astype(F32)
    named = jnp.zeros((count_tok, experts), F32)
    weight = jnp.zeros((count_tok, experts), F32)
    for k in range(chosen):
        hit = routes[:, k : k + 1] == expert_ids
        where = jnp.sum(jnp.where(hit, spot, 0.0), axis=1, keepdims=True)
        mine = where == expert_ids_f
        named = jnp.where(mine, 1.0, named)
        weight = jnp.where(mine, route_weight[:, k : k + 1], weight)
    before = (
        lax.broadcasted_iota(jnp.int32, (count_tok, count_tok), 0)
        > lax.broadcasted_iota(jnp.int32, (count_tok, count_tok), 1)
    ).astype(BF)
    rank = matmul(before, named.astype(BF))

    for r in range(2):
        chosen_rank = rank < 0.5 if r == 0 else rank > 0.5
        pick = jnp.where(chosen_rank, named, 0.0)
        select[r] = pick.astype(BF)
        row_weight = jnp.sum(pick * weight, axis=0, keepdims=True)
        row_weight = jnp.transpose(jnp.broadcast_to(row_weight, (LANES, experts)))
        token_rows = matmul(select[r], tokens[...], 0, 0)
        grad_rows = matmul(select[r], out_grad[...], 0, 0)
        for j in range(chunks):
            lanes = slice(j * LANES, (j + 1) * LANES)
            spread[r, pl.ds(j, experts, stride=units), :] = token_rows[:, lanes]
            spread[r, pl.ds(chunks + j, experts, stride=units), :] = (
                row_weight * grad_rows[:, lanes]
            )
        ready = spread[r].astype(BF).reshape(2, n, n, units, LANES)
        send0[r] = ready[0]
        send1[r] = ready[1]

    pl.semaphore_wait(barrier, len(greeted))

    for r in range(2):
        for i in range(1, n):
            yy, zz = turn(y, i), turn(z, i)
            remote(
                send0.at[r, yy], mid0.at[r, y], s1_send.at[r, 0], s1_recv.at[r, 0], at(yy, z, c)
            ).start()
            remote(
                send1.at[r, zz], mid1.at[r, z], s1_send.at[r, 1], s1_recv.at[r, 1], at(y, zz, c)
            ).start()
        mid0[r, y] = send0[r, y]
        mid1[r, z] = send1[r, z]

    some = at(y, z, 1 - c)
    for r in range(2):
        for p, (sent, mid) in enumerate(((send0, mid0), (send1, mid1))):
            if n > 1:
                part = pl.ds(0, n - 1)
                remote(
                    sent.at[r, part], mid.at[r, part], s1_send.at[r, p], s1_recv.at[r, p], some
                ).wait()
            base, slot = ((z, z * 2 + c), (y, y * 2 + c))[p]
            for i in range(1, n):
                other = turn(base, i)
                device = at(y, other, 0) if p == 0 else at(other, z, 1)
                remote(
                    mid.at[r, :, other], recv.at[r, slot], s2_send.at[r], s2_recv.at[r], device
                ).start()

            @pl.when(c == p)
            def _():
                recv[r, slot] = mid[r, :, base]

            @pl.when(c != p)
            def _():
                remote(
                    mid.at[r, :, base], recv.at[r, slot], s2_send.at[r], s2_recv.at[r], some
                ).start()

    for r in range(2):
        part = pl.ds(0, 2 * n - 1)
        remote(recv.at[r, part], recv.at[r, part], s2_send.at[r], s2_recv.at[r], some).wait()
        spread[r] = recv[r].reshape(experts * units, LANES).astype(F32)
        rows = slice(r * experts, (r + 1) * experts)
        for j in range(chunks):
            lanes = slice(j * LANES, (j + 1) * LANES)
            rows_all[rows, lanes] = spread[r, pl.ds(j, experts, stride=units), :].astype(BF)
            grad_all[rows, lanes] = spread[r, pl.ds(chunks + j, experts, stride=units), :].astype(BF)
        if r == 0:
            for load in loads:
                load.wait()
        shape = (parts, span, hidden_dim)
        psend[r, :, :, 0:hidden_dim] = (
            matmul(rows_all[rows, :], gate[...]).astype(BF).reshape(shape)
        )
        psend[r, :, :, hidden_dim : 2 * hidden_dim] = (
            matmul(rows_all[rows, :], up[...]).astype(BF).reshape(shape)
        )
        psend[r, :, :, 2 * hidden_dim :] = (
            matmul(grad_all[rows, :], down[...], 1, 1).astype(BF).reshape(shape)
        )
        for i in range(1, parts):
            q = lax.rem(d + i, parts)
            remote(
                psend.at[r, q], precv.at[r, i - 1], p_send.at[r, i - 1], p_recv.at[r, i - 1],
                {"dp": q},
            ).start()

    for r in range(2):
        total = psend[r, d].astype(F32)
        for i in range(1, parts):
            remote(
                psend.at[r, i], precv.at[r, i - 1], p_send.at[r, i - 1], p_recv.at[r, i - 1],
                {"dp": lax.rem(d + i, parts)},
            ).wait()
            total = total + precv[r, i - 1].astype(F32)
        gate_sum = total[:, 0:hidden_dim]
        up_sum = total[:, hidden_dim : 2 * hidden_dim]
        hidden_grad = total[:, 2 * hidden_dim :]
        sigma = jax.nn.sigmoid(gate_sum)
        active = gate_sum * sigma
        full[r, d, :, 0:hidden_dim] = (active * up_sum).astype(BF)
        full[r, d, :, hidden_dim : 2 * hidden_dim] = (
            hidden_grad * up_sum * sigma * (1.0 + gate_sum * (1.0 - sigma))
        ).astype(BF)
        full[r, d, :, 2 * hidden_dim :] = (hidden_grad * active).astype(BF)
        for i in range(1, parts):
            remote(
                full.at[r, d], full.at[r, d], a_send.at[r, i - 1], a_recv.at[r, i - 1],
                {"dp": lax.rem(d + i, parts)},
            ).start()

    for r in range(2):
        for i in range(1, parts):
            q = lax.rem(d + parts - i, parts)
            remote(
                full.at[r, q], full.at[r, q], a_send.at[r, i - 1], a_recv.at[r, i - 1], {"dp": q}
            ).wait()
        gate_back = full[r, :, :, hidden_dim : 2 * hidden_dim].reshape(experts, hidden_dim)
        up_back = full[r, :, :, 2 * hidden_dim :].reshape(experts, hidden_dim)
        row_back = matmul(gate_back, gate[...], 1, 1) + matmul(up_back, up[...], 1, 1)
        for j in range(chunks):
            spread[0, pl.ds(r * chunks + j, experts, stride=units), :] = row_back[
                :, j * LANES : (j + 1) * LANES
            ]
    ret[...] = spread[0].astype(BF).reshape(2 * n, n, units, LANES)

    base = jnp.where(c == 0, z, y)
    own = base * 2 + c
    back = c * n + base
    for i in range(1, 2 * n):
        j = lax.rem(own + i, 2 * n)
        jj, jc = j // 2, lax.rem(j, 2)
        device = at(jnp.where(c == 0, y, jj), jnp.where(c == 0, jj, z), jc)
        remote(ret.at[j], rmid.at[back], r1_send, r1_recv, device).start()
    rmid[back] = ret[own]

    stores = []
    for i, (left, first, result, out) in enumerate(
        ((rows_all, 1, gate_grad, gate_grad_hbm), (rows_all, 2, up_grad, up_grad_hbm))
    ):
        right = full[:, :, :, first * hidden_dim : (first + 1) * hidden_dim]
        result[...] = matmul(left[...], right.reshape(2 * experts, hidden_dim), 0, 0).astype(BF)
        stores.append(pltpu.make_async_copy(result, out.at[0], store_sem.at[i]))
        stores[-1].start()
    hidden = full[:, :, :, 0:hidden_dim].reshape(2 * experts, hidden_dim)
    down_grad[...] = matmul(hidden, grad_all[...], 0, 0).astype(BF)
    stores.append(pltpu.make_async_copy(down_grad, down_grad_hbm.at[0], store_sem.at[2]))
    stores[-1].start()

    part = pl.ds(0, 2 * n - 1)
    remote(ret.at[part], rmid.at[part], r1_send, r1_recv, some).wait()
    for i in range(1, n):
        yy, zz = turn(y, i), turn(z, i)
        remote(
            rmid.at[pl.ds(0, n), yy], fin0.at[y], r2_send.at[0], r2_recv.at[0], at(yy, z, c)
        ).start()
        remote(
            rmid.at[pl.ds(n, n), zz], fin1.at[z], r2_send.at[1], r2_recv.at[1], at(y, zz, c)
        ).start()
    fin0[y] = rmid[0:n, y]
    fin1[z] = rmid[n : 2 * n, z]
    if n > 1:
        part = pl.ds(0, n - 1)
        for p, fin in enumerate((fin0, fin1)):
            remote(fin.at[part], fin.at[part], r2_send.at[p], r2_recv.at[p], some).wait()

    half = n * n * units
    spread[1, 0:half, :] = fin0[...].reshape(half, LANES).astype(F32)
    spread[1, half : 2 * half, :] = fin1[...].reshape(half, LANES).astype(F32)
    for j in range(chunks):
        total = jnp.zeros((count_tok, LANES), F32)
        for r in range(2):
            came = spread[1, pl.ds(r * chunks + j, experts, stride=units), :].astype(BF)
            total = total + matmul(select[r], came)
        in_grad[:, j * LANES : (j + 1) * LANES] = total.astype(BF)
    for store in stores:
        store.wait()


def local(tokens, out_grad, routes, route_weight, placement, gate_weight, up_weight, down_weight):
    experts = lax.axis_size("expert")
    parts = lax.axis_size("dp")
    side = 1
    while 2 * side * side < experts:
        side *= 2
    n = side
    count_tok, width = tokens.shape
    _, _, hidden_dim = gate_weight.shape
    units = 2 * width // LANES
    span = experts // parts
    vmem = pl.BlockSpec(memory_space=pltpu.VMEM)
    hbm = pl.BlockSpec(memory_space=pl.ANY)
    dma = pltpu.SemaphoreType.DMA

    def buf(*shape, dtype=BF):
        return pltpu.VMEM(shape, dtype)

    return pl.pallas_call(
        functools.partial(kernel, side, parts),
        out_shape=(
            jax.ShapeDtypeStruct((count_tok, width), BF),
            jax.ShapeDtypeStruct(gate_weight.shape, BF),
            jax.ShapeDtypeStruct(up_weight.shape, BF),
            jax.ShapeDtypeStruct(down_weight.shape, BF),
        ),
        in_specs=[vmem] * 5 + [hbm] * 3,
        out_specs=(vmem, hbm, hbm, hbm),
        scratch_shapes=[
            buf(width, hidden_dim), buf(width, hidden_dim), buf(hidden_dim, width),
            buf(width, hidden_dim), buf(width, hidden_dim), buf(hidden_dim, width),
            buf(2, n, n, units, LANES), buf(2, n, n, units, LANES),
            buf(2, n, n, units, LANES), buf(2, n, n, units, LANES),
            buf(2, 2 * n, n, units, LANES),
            buf(2 * experts, width), buf(2 * experts, width),
            buf(2, parts, span, 3 * hidden_dim),
            buf(2, parts - 1, span, 3 * hidden_dim),
            buf(2, parts, span, 3 * hidden_dim),
            buf(2 * n, n, units, LANES), buf(2 * n, n, units, LANES),
            buf(n, n, units, LANES), buf(n, n, units, LANES),
            buf(2, experts * units, LANES, dtype=F32),
            buf(2, count_tok, experts),
            dma((3,)), dma((3,)),
            dma((2, 2)), dma((2, 2)), dma((2,)), dma((2,)),
            dma((2, parts - 1)), dma((2, parts - 1)), dma((2, parts - 1)), dma((2, parts - 1)),
            dma, dma, dma((2,)), dma((2,)),
        ],
        compiler_params=pltpu.CompilerParams(
            collective_id=0, has_side_effects=True, vmem_limit_bytes=48 << 20
        ),
        name="expert_backward",
    )(
        tokens, out_grad, routes, route_weight, placement.reshape(1, experts),
        gate_weight, up_weight, down_weight,
    )


def solution(mesh):
    in_specs = (
        P("expert", "dp"),
        P("expert", "dp"),
        P("expert", None),
        P("expert", None),
        P(),
        P("expert", "dp", None),
        P("expert", "dp", None),
        P("expert", None, "dp"),
    )
    out_specs = (
        P("expert", "dp"),
        P("expert", "dp", None),
        P("expert", "dp", None),
        P("expert", None, "dp"),
    )
    return jax.shard_map(local, mesh=mesh, in_specs=in_specs, out_specs=out_specs, check_vma=False)
```

```python
import functools

import jax
import jax.numpy as jnp
from jax import lax
from jax.experimental import pallas as pl
from jax.experimental.pallas import tpu as pltpu
from jax.sharding import PartitionSpec as P

BF = jnp.bfloat16
F32 = jnp.float32
LANES = 128
PARTS = 4


def matmul(left, right, left_dim=1, right_dim=0):
    return lax.dot_general(
        left, right, (((left_dim,), (right_dim,)), ((), ())), preferred_element_type=F32
    )


def remote(src, dst, send_sem, recv_sem, device):
    return pltpu.make_async_remote_copy(
        src_ref=src,
        dst_ref=dst,
        send_sem=send_sem,
        recv_sem=recv_sem,
        device_id=device,
        device_id_type=pl.DeviceIdType.MESH,
    )


def kernel(
    side,
    tokens_hbm, out_grad_hbm, routes_hbm, weight_hbm, placement_hbm, gate_hbm, up_hbm, down_hbm,
    in_grad_hbm, gate_grad_hbm, up_grad_hbm, down_grad_hbm,
    tokens, out_grad, routes, route_weight, placement, gate, up, down,
    in_grad, gate_grad, up_grad, down_grad,
    send0, send1, mid0, mid1, recv, rows_all, grad_all,
    psend, psum, prel, precv, full, hid, ret, rmid, fin0, fin1, wide, narrow, select,
    load_sem, store_sem, go_sem, s1_send, s1_recv, s2_send, s2_recv,
    p_send, p_recv, a_send, a_recv, h_send, h_recv, r1_send, r1_recv, r2_send, r2_recv,
):
    n = side
    block = n * n
    experts = 2 * block
    count_tok, width = tokens.shape
    chunks = width // LANES
    units = 2 * chunks
    hidden_dim = gate.shape[1]
    chosen = routes.shape[0]
    span = experts // PARTS
    me = lax.axis_index("expert")
    d = lax.axis_index("dp")
    y = me // (2 * n)
    z = lax.rem(me // 2, n)
    c = lax.rem(me, 2)

    def at(yy, zz, cc):
        return {"expert": (yy * n + zz) * 2 + cc}

    def turn(base, i):
        return lax.rem(base + i, n)

    sibling = at(y, z, 1 - c)

    loads = [
        pltpu.make_async_copy(src, dst, load_sem.at[i])
        for i, (src, dst) in enumerate(
            (
                (placement_hbm, placement), (routes_hbm, routes), (weight_hbm, route_weight),
                (tokens_hbm, tokens), (out_grad_hbm, out_grad),
                (gate_hbm.at[0], gate), (up_hbm.at[0], up), (down_hbm.at[0], down),
            )
        )
    ]
    for load in loads:
        load.start()

    barrier = pltpu.get_barrier_semaphore()
    greeted = [sibling]
    for i in range(1, n):
        for cc in range(2):
            greeted += [at(turn(y, i), z, cc), at(y, turn(z, i), cc)]
    right, left = lax.rem(d + 1, PARTS), lax.rem(d + PARTS - 1, PARTS)
    opposite = lax.rem(d + 2, PARTS)
    greeted += [{"dp": right}, {"dp": left}, {"dp": opposite}]
    for device in greeted:
        pl.semaphore_signal(
            barrier, inc=1, device_id=device, device_id_type=pl.DeviceIdType.MESH
        )
    for load in loads[:5]:
        load.wait()

    place = placement[...]
    place_y, place_z, place_c = place // (2 * n), lax.rem(place // 2, n), lax.rem(place, 2)
    spot = jnp.where(place_c == 0, place_y * n + place_z, block + place_z * n + place_y)
    spot = jnp.transpose(jnp.broadcast_to(spot.astype(F32), (LANES, experts)))[:, :count_tok]
    expert_ids = lax.broadcasted_iota(jnp.int32, (experts, count_tok), 0)
    expert_ids_f = expert_ids.astype(F32)
    named = jnp.zeros((experts, count_tok), F32)
    weight = jnp.zeros((experts, count_tok), F32)
    for k in range(chosen):
        hit = routes[k : k + 1, :] == expert_ids
        where = jnp.sum(jnp.where(hit, spot, 0.0), axis=0, keepdims=True)
        mine = where == expert_ids_f
        named = jnp.where(mine, 1.0, named)
        weight = jnp.where(mine, route_weight[k : k + 1, :], weight)
    before = (
        lax.broadcasted_iota(jnp.int32, (count_tok, count_tok), 0)
        < lax.broadcasted_iota(jnp.int32, (count_tok, count_tok), 1)
    ).astype(BF)
    rank = matmul(named.astype(BF), before)

    for r in range(2):
        chosen_rank = rank < 0.5 if r == 0 else rank > 0.5
        pick = jnp.where(chosen_rank, named, 0.0)
        select[r] = pick.astype(BF)
        row_weight = jnp.sum(pick * weight, axis=1, keepdims=True)
        token_rows = matmul(select[r], tokens[...])
        grad_rows = matmul(select[r], out_grad[...])
        for j in range(chunks):
            lanes = slice(j * LANES, (j + 1) * LANES)
            wide[pl.ds(r * units + j, experts, stride=2 * units), :] = token_rows[:, lanes]
            wide[pl.ds(r * units + chunks + j, experts, stride=2 * units), :] = (
                row_weight * grad_rows[:, lanes]
            )
    ready = wide[...].astype(BF).reshape(2, n, n, 2 * units, LANES)
    send0[...] = ready[0]
    send1[...] = ready[1]

    pl.semaphore_wait(barrier, len(greeted))

    @pl.when(c == 1)
    def _():
        pl.semaphore_wait(go_sem, 1)

    lines = ((send0, mid0, y), (send1, mid1, z))
    for i in range(1, n):
        for p, (sent, mid, base) in enumerate(lines):
            other = turn(base, i)
            device = at(other, z, c) if p == 0 else at(y, other, c)
            remote(sent.at[other], mid.at[base], s1_send.at[p], s1_recv.at[p], device).start()
    for sent, mid, base in lines:
        mid[base] = sent[base]
    if n > 1:
        most = pl.ds(0, n - 1)
        for p, (sent, mid, base) in enumerate(lines):
            remote(sent.at[most], mid.at[most], s1_send.at[p], s1_recv.at[p], sibling).wait_send()

    @pl.when(c == 0)
    def _():
        pl.semaphore_signal(
            go_sem, inc=1, device_id=sibling, device_id_type=pl.DeviceIdType.MESH
        )

    for p, (sent, mid, slot) in enumerate(lines):
        base = z if p == 0 else y
        if n > 1:
            remote(sent.at[most], mid.at[most], s1_send.at[p], s1_recv.at[p], sibling).wait_recv()
        for i in range(1, n):
            other = turn(base, i)
            device = at(y, other, 0) if p == 0 else at(other, z, 1)
            remote(
                mid.at[:, other], recv.at[c, base], s2_send, s2_recv.at[c], device
            ).start()

        @pl.when(c == p)
        def _():
            recv[c, base] = mid[:, base]

        @pl.when(c != p)
        def _():
            remote(
                mid.at[:, base], recv.at[c, base], s2_send, s2_recv.at[c], sibling
            ).start()

    half = span // 2
    first, second = pl.ds(0, half), pl.ds(half, half)

    def hop(src, dst, sems, h, i, device):
        send_sem, recv_sem = sems
        return remote(src, dst, send_sem.at[h, i], recv_sem.at[h, i], {"dp": device})

    def sums(h, i):
        src, dst, device = (
            lambda: (psend.at[h, opposite, first], prel.at[h, 0], right),
            lambda: (psend.at[h, opposite, second], prel.at[h, 1], left),
            lambda: (psend.at[h, right, second], precv.at[h, 0, second], right),
            lambda: (psend.at[h, left, first], precv.at[h, 1, first], left),
            lambda: (psum.at[h, 0], precv.at[h, 0, first], right),
            lambda: (psum.at[h, 1], precv.at[h, 1, second], left),
        )[i]()
        return hop(src, dst, (p_send, p_recv), h, i, device)

    def gathers(h, i):
        owner, part, device = (
            (d, first, right), (d, second, left), (d, second, right), (d, first, left),
            (left, first, right), (right, second, left),
        )[i]
        piece = full.at[h, owner, part]
        return hop(piece, piece, (a_send, a_recv), h, i, device)

    def gathered(h, i):
        owner, part = (
            (left, first), (right, second), (left, second), (right, first),
            (opposite, first), (opposite, second),
        )[i]
        piece = full.at[h, owner, part]
        return hop(piece, piece, (a_send, a_recv), h, i, right)

    def hidden_copy(h, i):
        owner = lax.rem(d + PARTS - i, PARTS)
        send_piece, piece = hid.at[h, d], hid.at[h, owner]
        return (
            hop(send_piece, send_piece, (h_send, h_recv), h, i - 1, lax.rem(d + i, PARTS)),
            hop(piece, piece, (h_send, h_recv), h, i - 1, lax.rem(d + i, PARTS)),
        )

    def partial_sums(h):
        for same in range(2):
            count = n - 1 if same else n
            if count:
                part = pl.ds(0, count)

                @pl.when((c == h) if same else (c != h))
                def _():
                    remote(
                        recv.at[h, part], recv.at[h, part], s2_send, s2_recv.at[h], sibling
                    ).wait_recv()

        rows = block * 2 * units
        wide[0:rows, :] = recv[h].reshape(rows, LANES).astype(F32)
        for r in range(2):
            start = h * experts + r * block
            for j in range(chunks):
                lanes = slice(j * LANES, (j + 1) * LANES)
                for kind, target in enumerate((rows_all, grad_all)):
                    offset = r * units + kind * chunks + j
                    target[start : start + block, lanes] = wide[
                        pl.ds(offset, block, stride=2 * units), :
                    ].astype(BF)
        if h == 0:
            for load in loads[5:]:
                load.wait()
        rows = slice(h * experts, (h + 1) * experts)
        shape = (PARTS, span, hidden_dim)
        psend[h, :, :, 0:hidden_dim] = (
            matmul(rows_all[rows, :], gate[...]).astype(BF).reshape(shape)
        )
        psend[h, :, :, hidden_dim : 2 * hidden_dim] = (
            matmul(rows_all[rows, :], up[...]).astype(BF).reshape(shape)
        )
        psend[h, :, :, 2 * hidden_dim :] = (
            matmul(grad_all[rows, :], down[...], 1, 1).astype(BF).reshape(shape)
        )
        for i in range(4):
            sums(h, i).start()

    def pass_sums(h):
        sums(h, 0).wait_recv()
        psum[h, 0] = (psend[h, right, first].astype(F32) + prel[h, 0].astype(F32)).astype(BF)
        sums(h, 4).start()
        sums(h, 1).wait_recv()
        psum[h, 1] = (psend[h, left, second].astype(F32) + prel[h, 1].astype(F32)).astype(BF)
        sums(h, 5).start()

    def activations(h):
        for i in range(2, 6):
            sums(h, i).wait_recv()
        total = (
            psend[h, d].astype(F32) + precv[h, 0].astype(F32) + precv[h, 1].astype(F32)
        )
        gate_sum = total[:, 0:hidden_dim]
        up_sum = total[:, hidden_dim : 2 * hidden_dim]
        hidden_grad = total[:, 2 * hidden_dim :]
        sigma = jax.nn.sigmoid(gate_sum)
        active = gate_sum * sigma
        full[h, d, :, 0:hidden_dim] = (
            hidden_grad * up_sum * sigma * (1.0 + gate_sum * (1.0 - sigma))
        ).astype(BF)
        full[h, d, :, hidden_dim:] = (hidden_grad * active).astype(BF)
        for i in range(4):
            gathers(h, i).start()
        hid[h, d] = (active * up_sum).astype(BF)

    def pass_gathers(h):
        gathered(h, 0).wait_recv()
        gathers(h, 4).start()
        gathered(h, 1).wait_recv()
        gathers(h, 5).start()

    def row_gradients(h):
        for i in range(2, 6):
            gathered(h, i).wait_recv()
        gate_back = full[h, :, :, 0:hidden_dim].reshape(experts, hidden_dim)
        up_back = full[h, :, :, hidden_dim:].reshape(experts, hidden_dim)
        row_back = matmul(gate_back, gate[...], 1, 1) + matmul(up_back, up[...], 1, 1)
        for r in range(2):
            for j in range(chunks):
                narrow[pl.ds(r * chunks + j, block, stride=units), :] = row_back[
                    r * block : (r + 1) * block, j * LANES : (j + 1) * LANES
                ]
        ret[h] = narrow[0 : block * units, :].astype(BF).reshape(n, n, units, LANES)

        base = jnp.where(c == 0, z, y)
        for i in range(n):
            other = turn(base, i)
            device = at(jnp.where(c == 0, y, other), jnp.where(c == 0, other, z), h)

            def go():
                remote(
                    ret.at[h, other], rmid.at[c, base], r1_send.at[h], r1_recv, device
                ).start()

            if i:
                go()
            else:
                pl.when(c != h)(go)

                @pl.when(c == h)
                def _():
                    rmid[c, base] = ret[h, base]

    def return_second():
        part = pl.ds(0, 2 * n - 1)
        mine = rmid.reshape(2 * n, n, units, LANES).at[part]
        remote(mine, mine, r1_send.at[0], r1_recv, sibling).wait_recv()
        for i in range(1, n):
            yy, zz = turn(y, i), turn(z, i)
            remote(
                rmid.at[0, :, yy], fin0.at[y], r2_send.at[0], r2_recv.at[0], at(yy, z, c)
            ).start()
            remote(
                rmid.at[1, :, zz], fin1.at[z], r2_send.at[1], r2_recv.at[1], at(y, zz, c)
            ).start()
        fin0[y] = rmid[0, :, y]
        fin1[z] = rmid[1, :, z]

    partial_sums(0)
    pass_sums(0)
    partial_sums(1)
    activations(0)
    pass_sums(1)
    pass_gathers(0)
    activations(1)
    pass_gathers(1)
    row_gradients(0)
    for h in range(2):
        for i in range(1, PARTS):
            hidden_copy(h, i)[0].start()
    row_gradients(1)
    pl.when(c == 0)(return_second)

    stores = []

    def store(i, src, dst):
        stores.append(pltpu.make_async_copy(src, dst, store_sem.at[i]))
        stores[-1].start()

    def weight_gradient(part, result, out):
        back = full[:, :, :, part * hidden_dim : (part + 1) * hidden_dim]
        back = back.reshape(2 * experts, hidden_dim)
        result[...] = matmul(rows_all[...], back, 0, 0).astype(BF)
        store(part, result, out.at[0])

    weight_gradient(0, gate_grad, gate_grad_hbm)
    pl.when(c == 1)(return_second)
    weight_gradient(1, up_grad, up_grad_hbm)
    for h in range(2):
        for i in range(1, PARTS):
            hidden_copy(h, i)[1].wait()
    hidden = hid[...].reshape(2 * experts, hidden_dim)
    down_grad[...] = matmul(hidden, grad_all[...], 0, 0).astype(BF)
    store(2, down_grad, down_grad_hbm.at[0])

    for h in range(2):
        for i in range(6):
            sums(h, i).wait_send()
            gathers(h, i).wait_send()
    for same in range(2):
        count = n - 1 if same else n
        for h in range(2):
            if count:
                part = pl.ds(0, count)

                @pl.when((c == h) if same else (c != h))
                def _():
                    remote(
                        ret.at[h, part], ret.at[h, part], r1_send.at[h], r1_recv, sibling
                    ).wait_send()

    part = pl.ds(0, 2 * n - 1)
    moved = recv.reshape(2 * n, n, 2 * units, LANES).at[part]
    remote(moved, moved, s2_send, s2_recv.at[0], sibling).wait_send()

    if n > 1:
        for p, fin in enumerate((fin0, fin1)):
            remote(fin.at[most], fin.at[most], r2_send.at[p], r2_recv.at[p], sibling).wait()
    whole = block * units
    narrow[0:whole, :] = fin0[...].reshape(whole, LANES).astype(F32)
    narrow[whole : 2 * whole, :] = fin1[...].reshape(whole, LANES).astype(F32)
    for j in range(chunks):
        total = jnp.zeros((count_tok, LANES), F32)
        for r in range(2):
            came = narrow[pl.ds(r * chunks + j, experts, stride=units), :].astype(BF)
            total = total + matmul(select[r], came, 0, 0)
        in_grad[:, j * LANES : (j + 1) * LANES] = total.astype(BF)
    store(3, in_grad, in_grad_hbm)
    for copy in stores:
        copy.wait()


def hand_over(*refs):
    count = (len(refs) - 2) // 3
    given, kept, passed = refs[:count], refs[count : 2 * count], refs[2 * count : 3 * count]
    come, go = refs[-2:]
    pieces = []
    for i in range(count):
        rows = given[i].shape[-2]
        step = max(rows // 4, min(rows, 32))
        for at in range(0, rows, step):
            part = (0, pl.ds(at, step)) if len(given[i].shape) == 3 else (pl.ds(at, step),)
            pieces.append((given[i].at[part], passed[i].at[part], kept[i].at[part]))
    reads = [pltpu.make_async_copy(src, mid, come.at[k]) for k, (src, mid, _) in enumerate(pieces)]
    writes = [pltpu.make_async_copy(mid, dst, go.at[k]) for k, (_, mid, dst) in enumerate(pieces)]
    for read in reads:
        read.start()
    for read, write in zip(reads, writes):
        read.wait()
        write.start()
    for write in writes:
        write.wait()


def local(tokens, out_grad, routes, route_weight, placement, gate_weight, up_weight, down_weight):
    experts = lax.axis_size("expert")
    side = 1
    while 2 * side * side < experts:
        side *= 2
    n = side
    count_tok, width = tokens.shape
    chosen = routes.shape[1]
    _, _, hidden_dim = gate_weight.shape
    units = 2 * width // LANES
    span = experts // PARTS
    hbm = pl.BlockSpec(memory_space=pltpu.HBM)
    dma = pltpu.SemaphoreType.DMA

    def buf(*shape, dtype=BF):
        return pltpu.VMEM(shape, dtype)

    shapes = (
        jax.ShapeDtypeStruct((count_tok, width), BF),
        jax.ShapeDtypeStruct(gate_weight.shape, BF),
        jax.ShapeDtypeStruct(up_weight.shape, BF),
        jax.ShapeDtypeStruct(down_weight.shape, BF),
    )
    results = pl.pallas_call(
        functools.partial(kernel, side),
        out_shape=shapes,
        in_specs=[hbm] * 8,
        out_specs=(hbm,) * 4,
        scratch_shapes=[
            buf(count_tok, width), buf(count_tok, width),
            buf(chosen, count_tok, dtype=jnp.int32), buf(chosen, count_tok, dtype=F32),
            buf(1, experts, dtype=jnp.int32),
            buf(width, hidden_dim), buf(width, hidden_dim), buf(hidden_dim, width),
            buf(count_tok, width),
            buf(width, hidden_dim), buf(width, hidden_dim), buf(hidden_dim, width),
            buf(n, n, 2 * units, LANES), buf(n, n, 2 * units, LANES),
            buf(n, n, 2 * units, LANES), buf(n, n, 2 * units, LANES),
            buf(2, n, n, 2 * units, LANES),
            buf(2 * experts, width), buf(2 * experts, width),
            buf(2, PARTS, span, 3 * hidden_dim),
            buf(2, 2, span // 2, 3 * hidden_dim),
            buf(2, 2, span // 2, 3 * hidden_dim),
            buf(2, 2, span, 3 * hidden_dim),
            buf(2, PARTS, span, 2 * hidden_dim),
            buf(2, PARTS, span, hidden_dim),
            buf(2, n, n, units, LANES), buf(2, n, n, units, LANES),
            buf(n, n, units, LANES), buf(n, n, units, LANES),
            buf(experts * 2 * units, LANES, dtype=F32),
            buf(experts * units, LANES, dtype=F32),
            buf(2, experts, count_tok),
            dma((8,)), dma((4,)), pltpu.SemaphoreType.REGULAR,
            dma((2,)), dma((2,)), dma, dma((2,)),
            dma((2, 6)), dma((2, 6)), dma((2, 6)), dma((2, 6)), dma((2, 3)), dma((2, 3)),
            dma((2,)), dma, dma((2,)), dma((2,)),
        ],
        compiler_params=pltpu.CompilerParams(
            collective_id=0, has_side_effects=True, vmem_limit_bytes=61 << 20
        ),
        name="expert_backward",
    )(
        tokens, out_grad, routes.T, route_weight.T, placement.reshape(1, experts),
        gate_weight, up_weight, down_weight,
    )
    return pl.pallas_call(
        hand_over,
        out_shape=shapes,
        in_specs=[hbm] * 4,
        out_specs=(hbm,) * 4,
        scratch_shapes=[buf(*shape.shape) for shape in shapes] + [dma((16,)), dma((16,))],
        compiler_params=pltpu.CompilerParams(vmem_limit_bytes=61 << 20),
        name="hand_over",
    )(*results)


def solution(mesh):
    in_specs = (
        P("expert", "dp"),
        P("expert", "dp"),
        P("expert", None),
        P("expert", None),
        P(),
        P("expert", "dp", None),
        P("expert", "dp", None),
        P("expert", None, "dp"),
    )
    out_specs = (
        P("expert", "dp"),
        P("expert", "dp", None),
        P("expert", "dp", None),
        P("expert", None, "dp"),
    )
    return jax.shard_map(local, mesh=mesh, in_specs=in_specs, out_specs=out_specs, check_vma=False)
```

```python
import functools

import jax
import jax.numpy as jnp
from jax import lax
from jax.experimental import pallas as pl
from jax.experimental.pallas import tpu as pltpu
from jax.sharding import PartitionSpec as P

BF = jnp.bfloat16
F32 = jnp.float32
LANES = 128
PARTS = 4


def matmul(left, right, left_dim=1, right_dim=0):
    return lax.dot_general(
        left, right, (((left_dim,), (right_dim,)), ((), ())), preferred_element_type=F32
    )


def remote(src, dst, send_sem, recv_sem, device):
    return pltpu.make_async_remote_copy(
        src_ref=src,
        dst_ref=dst,
        send_sem=send_sem,
        recv_sem=recv_sem,
        device_id=device,
        device_id_type=pl.DeviceIdType.MESH,
    )


def kernel(
    side,
    tokens_hbm, out_grad_hbm, routes_hbm, weight_hbm, placement_hbm, gate_hbm, up_hbm, down_hbm,
    in_grad_hbm, gate_grad_hbm, up_grad_hbm, down_grad_hbm,
    tokens, out_grad, routes, route_weight, placement, gate, up, down,
    in_grad, gate_grad, up_grad, down_grad,
    send0, send1, mid0, mid1, recv, rows_all, grad_all,
    turned, psend, psum, prel, precv, full, hid, ret, fin, wide, narrow, select,
    load_sem, store_sem, go_sem, s1_send, s1_recv, s2_send, s2_recv,
    p_send, p_recv, a_send, a_recv, h_send, h_recv, r_send, r_recv,
):
    n = side
    block = n * n
    experts = 2 * block
    count_tok, width = tokens.shape
    chunks = width // LANES
    units = 2 * chunks
    hidden_dim = gate.shape[1]
    chosen = routes.shape[0]
    span = experts // PARTS
    me = lax.axis_index("expert")
    d = lax.axis_index("dp")
    y = me // (2 * n)
    z = lax.rem(me // 2, n)
    c = lax.rem(me, 2)

    def at(yy, zz, cc):
        return {"expert": (yy * n + zz) * 2 + cc}

    def turn(base, i):
        return jnp.bitwise_and(base + i, n - 1)

    offsets = sorted(range(n), key=lambda i: (-min(i, n - i), i))

    sibling = at(y, z, 1 - c)

    loads = [
        pltpu.make_async_copy(src, dst, load_sem.at[i])
        for i, (src, dst) in enumerate(
            (
                (placement_hbm, placement), (routes_hbm, routes), (weight_hbm, route_weight),
                (tokens_hbm, tokens), (out_grad_hbm, out_grad),
                (gate_hbm.at[0], gate), (up_hbm.at[0], up), (down_hbm.at[0], down),
            )
        )
    ]
    for load in loads:
        load.start()

    barrier = pltpu.get_barrier_semaphore()
    greeted = [sibling]
    for i in range(1, n):
        for cc in range(2):
            greeted += [at(turn(y, i), z, cc), at(y, turn(z, i), cc)]
    right, left = lax.rem(d + 1, PARTS), lax.rem(d + PARTS - 1, PARTS)
    opposite = lax.rem(d + 2, PARTS)
    greeted += [{"dp": right}, {"dp": left}, {"dp": opposite}]
    for device in greeted:
        pl.semaphore_signal(
            barrier, inc=1, device_id=device, device_id_type=pl.DeviceIdType.MESH
        )
    for load in loads[:5]:
        load.wait()

    place = placement[...]
    place_y, place_z, place_c = place // (2 * n), lax.rem(place // 2, n), lax.rem(place, 2)
    spot = jnp.where(place_c == 0, place_y * n + place_z, block + place_z * n + place_y)
    spot = jnp.transpose(jnp.broadcast_to(spot.astype(F32), (LANES, experts)))[:, :count_tok]
    expert_ids = lax.broadcasted_iota(jnp.int32, (experts, count_tok), 0)
    expert_ids_f = expert_ids.astype(F32)
    named = jnp.zeros((experts, count_tok), F32)
    weight = jnp.zeros((experts, count_tok), F32)
    for k in range(chosen):
        hit = routes[k : k + 1, :] == expert_ids
        where = jnp.sum(jnp.where(hit, spot, 0.0), axis=0, keepdims=True)
        mine = where == expert_ids_f
        named = jnp.where(mine, 1.0, named)
        weight = jnp.where(mine, route_weight[k : k + 1, :], weight)
    before = (
        lax.broadcasted_iota(jnp.int32, (count_tok, count_tok), 0)
        < lax.broadcasted_iota(jnp.int32, (count_tok, count_tok), 1)
    ).astype(BF)
    rank = matmul(named.astype(BF), before)

    for r in range(2):
        chosen_rank = rank < 0.5 if r == 0 else rank > 0.5
        pick = jnp.where(chosen_rank, named, 0.0)
        select[r] = pick.astype(BF)
        row_weight = jnp.sum(pick * weight, axis=1, keepdims=True)
        token_rows = matmul(select[r], tokens[...])
        grad_rows = matmul(select[r], out_grad[...])
        for j in range(chunks):
            lanes = slice(j * LANES, (j + 1) * LANES)
            wide[pl.ds(r * units + j, experts, stride=2 * units), :] = token_rows[:, lanes]
            wide[pl.ds(r * units + chunks + j, experts, stride=2 * units), :] = (
                row_weight * grad_rows[:, lanes]
            )
    ready = wide[...].astype(BF).reshape(2, n, n, 2 * units, LANES)
    send0[...] = ready[0]
    send1[...] = ready[1]

    pl.semaphore_wait(barrier, len(greeted))

    @pl.when(c == 1)
    def _():
        pl.semaphore_wait(go_sem, 1)

    lines = ((send0, mid0, y), (send1, mid1, z))
    for i in offsets[:-1]:
        for p, (sent, mid, base) in enumerate(lines):
            other = turn(base, i)
            device = at(other, z, c) if p == 0 else at(y, other, c)
            remote(sent.at[other], mid.at[base], s1_send.at[p], s1_recv.at[p], device).start()
    for sent, mid, base in lines:
        mid[base] = sent[base]
    if n > 1:
        most = pl.ds(0, n - 1)
        for p, (sent, mid, base) in enumerate(lines):
            remote(sent.at[most], mid.at[most], s1_send.at[p], s1_recv.at[p], sibling).wait_send()

    @pl.when(c == 0)
    def _():
        pl.semaphore_signal(
            go_sem, inc=1, device_id=sibling, device_id_type=pl.DeviceIdType.MESH
        )

    for p, (sent, mid, slot) in enumerate(lines):
        base = z if p == 0 else y
        if n > 1:
            remote(sent.at[most], mid.at[most], s1_send.at[p], s1_recv.at[p], sibling).wait_recv()
        for i in range(n):
            for j in range(n):
                turned[p, i, j] = mid[j, i]
        for i in offsets[:-1]:
            other = turn(base, i)
            device = at(y, other, 0) if p == 0 else at(other, z, 1)
            remote(
                turned.at[p, other], recv.at[c, base], s2_send, s2_recv.at[c], device
            ).start()

        @pl.when(c == p)
        def _():
            recv[c, base] = turned[p, base]

        @pl.when(c != p)
        def _():
            remote(
                turned.at[p, base], recv.at[c, base], s2_send, s2_recv.at[c], sibling
            ).start()

    half = span // 2
    first, second = pl.ds(0, half), pl.ds(half, half)

    def hop(src, dst, sems, h, i, device):
        send_sem, recv_sem = sems
        return remote(src, dst, send_sem.at[h, i], recv_sem.at[h, i], {"dp": device})

    def sums(h, i):
        src, dst, device = (
            lambda: (psend.at[h, opposite, first], prel.at[h, 0], right),
            lambda: (psend.at[h, opposite, second], prel.at[h, 1], left),
            lambda: (psend.at[h, right, second], precv.at[h, 0, second], right),
            lambda: (psend.at[h, left, first], precv.at[h, 1, first], left),
            lambda: (psum.at[h, 0], precv.at[h, 0, first], right),
            lambda: (psum.at[h, 1], precv.at[h, 1, second], left),
        )[i]()
        return hop(src, dst, (p_send, p_recv), h, i, device)

    def gathers(h, i):
        owner, part, device = (
            (d, first, right), (d, second, left), (d, second, right), (d, first, left),
            (left, first, right), (right, second, left),
        )[i]
        piece = full.at[h, owner, part]
        return hop(piece, piece, (a_send, a_recv), h, i, device)

    def gathered(h, i):
        owner, part = (
            (left, first), (right, second), (left, second), (right, first),
            (opposite, first), (opposite, second),
        )[i]
        piece = full.at[h, owner, part]
        return hop(piece, piece, (a_send, a_recv), h, i, right)

    def hidden_copy(h, i):
        owner = lax.rem(d + PARTS - i, PARTS)
        send_piece, piece = hid.at[h, d], hid.at[h, owner]
        return (
            hop(send_piece, send_piece, (h_send, h_recv), h, i - 1, lax.rem(d + i, PARTS)),
            hop(piece, piece, (h_send, h_recv), h, i - 1, lax.rem(d + i, PARTS)),
        )

    def partial_sums(h):
        for same in range(2):
            count = n - 1 if same else n
            if count:
                part = pl.ds(0, count)

                @pl.when((c == h) if same else (c != h))
                def _():
                    remote(
                        recv.at[h, part], recv.at[h, part], s2_send, s2_recv.at[h], sibling
                    ).wait_recv()

        rows = block * 2 * units
        wide[0:rows, :] = recv[h].reshape(rows, LANES).astype(F32)
        for r in range(2):
            start = h * experts + r * block
            for j in range(chunks):
                lanes = slice(j * LANES, (j + 1) * LANES)
                for kind, target in enumerate((rows_all, grad_all)):
                    offset = r * units + kind * chunks + j
                    target[start : start + block, lanes] = wide[
                        pl.ds(offset, block, stride=2 * units), :
                    ].astype(BF)
        if h == 0:
            for load in loads[5:]:
                load.wait()
        rows = slice(h * experts, (h + 1) * experts)
        shape = (PARTS, span, hidden_dim)
        psend[h, :, :, 0:hidden_dim] = (
            matmul(rows_all[rows, :], gate[...]).astype(BF).reshape(shape)
        )
        psend[h, :, :, hidden_dim : 2 * hidden_dim] = (
            matmul(rows_all[rows, :], up[...]).astype(BF).reshape(shape)
        )
        psend[h, :, :, 2 * hidden_dim :] = (
            matmul(grad_all[rows, :], down[...], 1, 1).astype(BF).reshape(shape)
        )
        for i in range(4):
            sums(h, i).start()

    def pass_sums(h):
        sums(h, 0).wait_recv()
        psum[h, 0] = (psend[h, right, first].astype(F32) + prel[h, 0].astype(F32)).astype(BF)
        sums(h, 4).start()
        sums(h, 1).wait_recv()
        psum[h, 1] = (psend[h, left, second].astype(F32) + prel[h, 1].astype(F32)).astype(BF)
        sums(h, 5).start()

    def activations(h):
        for i in range(2, 6):
            sums(h, i).wait_recv()
        total = (
            psend[h, d].astype(F32) + precv[h, 0].astype(F32) + precv[h, 1].astype(F32)
        )
        gate_sum = total[:, 0:hidden_dim]
        up_sum = total[:, hidden_dim : 2 * hidden_dim]
        hidden_grad = total[:, 2 * hidden_dim :]
        sigma = jax.nn.sigmoid(gate_sum)
        active = gate_sum * sigma
        full[h, d, :, 0:hidden_dim] = (
            hidden_grad * up_sum * sigma * (1.0 + gate_sum * (1.0 - sigma))
        ).astype(BF)
        full[h, d, :, hidden_dim:] = (hidden_grad * active).astype(BF)
        for i in range(4):
            gathers(h, i).start()
        hid[h, d] = (active * up_sum).astype(BF)

    def pass_gathers(h):
        gathered(h, 0).wait_recv()
        gathers(h, 4).start()
        gathered(h, 1).wait_recv()
        gathers(h, 5).start()

    def row_gradients(h):
        for i in range(2, 6):
            gathered(h, i).wait_recv()
        gate_back = full[h, :, :, 0:hidden_dim].reshape(experts, hidden_dim)
        up_back = full[h, :, :, hidden_dim:].reshape(experts, hidden_dim)
        row_back = matmul(gate_back, gate[...], 1, 1) + matmul(up_back, up[...], 1, 1)
        for r in range(2):
            for j in range(chunks):
                narrow[pl.ds(r * chunks + j, block, stride=units), :] = row_back[
                    r * block : (r + 1) * block, j * LANES : (j + 1) * LANES
                ]
        ret[h] = narrow[0 : block * units, :].astype(BF).reshape(n, n, units, LANES)

    def give_back(h):
        along, across = jnp.where(c == 0, z, y), jnp.where(c == 0, y, z)
        slots = [turn(along, i) for i in offsets]
        others = [turn(across, i) for i in offsets]
        to_slot = [slot * jnp.where(c == 0, 2, 2 * n) + h for slot in slots]
        to_other = [other * jnp.where(c == 0, 2 * n, 2) for other in others]
        for i, slot in enumerate(slots):
            for k, other in enumerate(others):
                copy = remote(
                    ret.at[h, slot, other], fin.at[c, across, along], r_send.at[h], r_recv,
                    {"expert": to_slot[i] + to_other[k]},
                )
                if offsets[i] or offsets[k]:
                    copy.start()
                else:
                    pl.when(c != h)(copy.start)

        @pl.when(c == h)
        def _():
            fin[c, across, along] = ret[h, along, across]

    partial_sums(0)
    pass_sums(0)
    partial_sums(1)
    activations(0)
    pass_sums(1)
    pass_gathers(0)
    activations(1)
    row_gradients(0)
    pass_gathers(1)
    give_back(0)
    row_gradients(1)
    give_back(1)
    for h in range(2):
        for i in range(1, PARTS):
            hidden_copy(h, i)[0].start()

    stores = []

    def store(i, src, dst):
        stores.append(pltpu.make_async_copy(src, dst, store_sem.at[i]))
        stores[-1].start()

    def weight_gradient(part, result, out):
        back = full[:, :, :, part * hidden_dim : (part + 1) * hidden_dim]
        back = back.reshape(2 * experts, hidden_dim)
        result[...] = matmul(rows_all[...], back, 0, 0).astype(BF)
        store(part, result, out.at[0])

    weight_gradient(0, gate_grad, gate_grad_hbm)
    weight_gradient(1, up_grad, up_grad_hbm)
    for h in range(2):
        for i in range(1, PARTS):
            hidden_copy(h, i)[1].wait()
    hidden = hid[...].reshape(2 * experts, hidden_dim)
    down_grad[...] = matmul(hidden, grad_all[...], 0, 0).astype(BF)
    store(2, down_grad, down_grad_hbm.at[0])

    for h in range(2):
        for i in range(6):
            sums(h, i).wait_send()
            gathers(h, i).wait_send()
    pieces = fin.reshape(experts, units, LANES)
    for same in range(2):
        count = block - 1 if same else block
        for h in range(2):
            if count:
                part = pieces.at[pl.ds(0, count)]

                @pl.when((c == h) if same else (c != h))
                def _():
                    remote(part, part, r_send.at[h], r_recv, sibling).wait_send()

    part = pl.ds(0, 2 * n - 1)
    moved = recv.reshape(2 * n, n, 2 * units, LANES).at[part]
    remote(moved, moved, s2_send, s2_recv.at[0], sibling).wait_send()

    part = pieces.at[pl.ds(0, experts - 1)]
    remote(part, part, r_send.at[0], r_recv, sibling).wait_recv()
    narrow[...] = fin[...].reshape(experts * units, LANES).astype(F32)
    for j in range(chunks):
        total = jnp.zeros((count_tok, LANES), F32)
        for r in range(2):
            came = narrow[pl.ds(r * chunks + j, experts, stride=units), :].astype(BF)
            total = total + matmul(select[r], came, 0, 0)
        in_grad[:, j * LANES : (j + 1) * LANES] = total.astype(BF)
    store(3, in_grad, in_grad_hbm)
    for copy in stores:
        copy.wait()


def hand_over(*refs):
    count = (len(refs) - 2) // 3
    given, kept, passed = refs[:count], refs[count : 2 * count], refs[2 * count : 3 * count]
    come, go = refs[-2:]
    pieces = []
    for i in range(count):
        rows = given[i].shape[-2]
        step = max(rows // 4, min(rows, 32))
        for at in range(0, rows, step):
            part = (0, pl.ds(at, step)) if len(given[i].shape) == 3 else (pl.ds(at, step),)
            pieces.append((given[i].at[part], passed[i].at[part], kept[i].at[part]))
    reads = [pltpu.make_async_copy(src, mid, come.at[k]) for k, (src, mid, _) in enumerate(pieces)]
    writes = [pltpu.make_async_copy(mid, dst, go.at[k]) for k, (_, mid, dst) in enumerate(pieces)]
    for read in reads:
        read.start()
    for read, write in zip(reads, writes):
        read.wait()
        write.start()
    for write in writes:
        write.wait()


def local(tokens, out_grad, routes, route_weight, placement, gate_weight, up_weight, down_weight):
    experts = lax.axis_size("expert")
    side = 1
    while 2 * side * side < experts:
        side *= 2
    n = side
    count_tok, width = tokens.shape
    chosen = routes.shape[1]
    _, _, hidden_dim = gate_weight.shape
    units = 2 * width // LANES
    span = experts // PARTS
    hbm = pl.BlockSpec(memory_space=pltpu.HBM)
    dma = pltpu.SemaphoreType.DMA

    def buf(*shape, dtype=BF):
        return pltpu.VMEM(shape, dtype)

    shapes = (
        jax.ShapeDtypeStruct((count_tok, width), BF),
        jax.ShapeDtypeStruct(gate_weight.shape, BF),
        jax.ShapeDtypeStruct(up_weight.shape, BF),
        jax.ShapeDtypeStruct(down_weight.shape, BF),
    )
    results = pl.pallas_call(
        functools.partial(kernel, side),
        out_shape=shapes,
        in_specs=[hbm] * 8,
        out_specs=(hbm,) * 4,
        scratch_shapes=[
            buf(count_tok, width), buf(count_tok, width),
            buf(chosen, count_tok, dtype=jnp.int32), buf(chosen, count_tok, dtype=F32),
            buf(1, experts, dtype=jnp.int32),
            buf(width, hidden_dim), buf(width, hidden_dim), buf(hidden_dim, width),
            buf(count_tok, width),
            buf(width, hidden_dim), buf(width, hidden_dim), buf(hidden_dim, width),
            buf(n, n, 2 * units, LANES), buf(n, n, 2 * units, LANES),
            buf(n, n, 2 * units, LANES), buf(n, n, 2 * units, LANES),
            buf(2, n, n, 2 * units, LANES),
            buf(2 * experts, width), buf(2 * experts, width),
            buf(2, n, n, 2 * units, LANES),
            buf(2, PARTS, span, 3 * hidden_dim),
            buf(2, 2, span // 2, 3 * hidden_dim),
            buf(2, 2, span // 2, 3 * hidden_dim),
            buf(2, 2, span, 3 * hidden_dim),
            buf(2, PARTS, span, 2 * hidden_dim),
            buf(2, PARTS, span, hidden_dim),
            buf(2, n, n, units, LANES), buf(2, n, n, units, LANES),
            buf(experts * 2 * units, LANES, dtype=F32),
            buf(experts * units, LANES, dtype=F32),
            buf(2, experts, count_tok),
            dma((8,)), dma((4,)), pltpu.SemaphoreType.REGULAR,
            dma((2,)), dma((2,)), dma, dma((2,)),
            dma((2, 6)), dma((2, 6)), dma((2, 6)), dma((2, 6)), dma((2, 3)), dma((2, 3)),
            dma((2,)), dma,
        ],
        compiler_params=pltpu.CompilerParams(
            collective_id=0, has_side_effects=True, vmem_limit_bytes=61 << 20
        ),
        name="expert_backward",
    )(
        tokens, out_grad, routes.T, route_weight.T, placement.reshape(1, experts),
        gate_weight, up_weight, down_weight,
    )
    return pl.pallas_call(
        hand_over,
        out_shape=shapes,
        in_specs=[hbm] * 4,
        out_specs=(hbm,) * 4,
        scratch_shapes=[buf(*shape.shape) for shape in shapes] + [dma((16,)), dma((16,))],
        compiler_params=pltpu.CompilerParams(vmem_limit_bytes=61 << 20),
        name="hand_over",
    )(*results)


def solution(mesh):
    in_specs = (
        P("expert", "dp"),
        P("expert", "dp"),
        P("expert", None),
        P("expert", None),
        P(),
        P("expert", "dp", None),
        P("expert", "dp", None),
        P("expert", None, "dp"),
    )
    out_specs = (
        P("expert", "dp"),
        P("expert", "dp", None),
        P("expert", "dp", None),
        P("expert", None, "dp"),
    )
    return jax.shard_map(local, mesh=mesh, in_specs=in_specs, out_specs=out_specs, check_vma=False)
```

```python
import functools

import jax
import jax.numpy as jnp
from jax import lax
from jax.experimental import pallas as pl
from jax.experimental.pallas import tpu as pltpu
from jax.sharding import PartitionSpec as P

BF = jnp.bfloat16
F32 = jnp.float32
LANES = 128
PARTS = 4


def matmul(left, right, left_dim=1, right_dim=0):
    return lax.dot_general(
        left, right, (((left_dim,), (right_dim,)), ((), ())), preferred_element_type=F32
    )


def remote(src, dst, send_sem, recv_sem, device):
    return pltpu.make_async_remote_copy(
        src_ref=src,
        dst_ref=dst,
        send_sem=send_sem,
        recv_sem=recv_sem,
        device_id=device,
        device_id_type=pl.DeviceIdType.MESH,
    )


def kernel(
    side,
    tokens_hbm, out_grad_hbm, routes_hbm, weight_hbm, placement_hbm, gate_hbm, up_hbm, down_hbm,
    in_grad_hbm, gate_grad_hbm, up_grad_hbm, down_grad_hbm,
    tokens, out_grad, routes, route_weight, placement, gate, up, down,
    in_grad, gate_grad, up_grad, down_grad,
    send0, send1, mid0, mid1, recv, rows_all, grad_all,
    turned, psend, psum, prel, precv, full, hid, ret, fin, wide, narrow, select,
    load_sem, store_sem, s1_send, s1_recv, s2_send, s2_recv,
    p_send, p_recv, a_send, a_recv, h_send, h_recv, r_send, r_recv,
):
    n = side
    block = n * n
    experts = 2 * block
    count_tok, width = tokens.shape
    chunks = width // LANES
    units = 2 * chunks
    hidden_dim = gate.shape[1]
    chosen = routes.shape[0]
    span = block // PARTS
    me = lax.axis_index("expert")
    d = lax.axis_index("dp")
    y = me // (2 * n)
    z = lax.rem(me // 2, n)
    c = lax.rem(me, 2)

    def at(yy, zz, cc):
        return {"expert": (yy * n + zz) * 2 + cc}

    def turn(base, i):
        return jnp.bitwise_and(base + i, n - 1)

    offsets = sorted(range(n), key=lambda i: (-min(i, n - i), i))

    sibling = at(y, z, 1 - c)

    loads = [
        pltpu.make_async_copy(src, dst, load_sem.at[i])
        for i, (src, dst) in enumerate(
            (
                (placement_hbm, placement), (routes_hbm, routes), (weight_hbm, route_weight),
                (tokens_hbm, tokens), (out_grad_hbm, out_grad),
                (gate_hbm.at[0], gate), (up_hbm.at[0], up), (down_hbm.at[0], down),
            )
        )
    ]
    for load in loads:
        load.start()

    barrier = pltpu.get_barrier_semaphore()
    greeted = [sibling]
    for i in range(1, n):
        for cc in range(2):
            greeted += [at(turn(y, i), z, cc), at(y, turn(z, i), cc)]
    right, left = lax.rem(d + 1, PARTS), lax.rem(d + PARTS - 1, PARTS)
    opposite = lax.rem(d + 2, PARTS)
    greeted += [{"dp": right}, {"dp": left}, {"dp": opposite}]
    for device in greeted:
        pl.semaphore_signal(
            barrier, inc=1, device_id=device, device_id_type=pl.DeviceIdType.MESH
        )
    for load in loads[:5]:
        load.wait()

    place = placement[...]
    place_y, place_z, place_c = place // (2 * n), lax.rem(place // 2, n), lax.rem(place, 2)
    spot = jnp.where(place_c == 0, place_y * n + place_z, block + place_z * n + place_y)
    spot = jnp.transpose(jnp.broadcast_to(spot.astype(F32), (LANES, experts)))[:, :count_tok]
    expert_ids = lax.broadcasted_iota(jnp.int32, (experts, count_tok), 0)
    expert_ids_f = expert_ids.astype(F32)
    named = jnp.zeros((experts, count_tok), F32)
    weight = jnp.zeros((experts, count_tok), F32)
    for k in range(chosen):
        hit = routes[k : k + 1, :] == expert_ids
        where = jnp.sum(jnp.where(hit, spot, 0.0), axis=0, keepdims=True)
        mine = where == expert_ids_f
        named = jnp.where(mine, 1.0, named)
        weight = jnp.where(mine, route_weight[k : k + 1, :], weight)
    before = (
        lax.broadcasted_iota(jnp.int32, (count_tok, count_tok), 0)
        < lax.broadcasted_iota(jnp.int32, (count_tok, count_tok), 1)
    ).astype(BF)
    rank = matmul(named.astype(BF), before)

    lines = ((send0, mid0, y), (send1, mid1, z))

    def prepare(r):
        chosen_rank = rank < 0.5 if r == 0 else rank > 0.5
        pick = jnp.where(chosen_rank, named, 0.0)
        select[r] = pick.astype(BF)
        row_weight = jnp.sum(pick * weight, axis=1, keepdims=True)
        token_rows = matmul(select[r], tokens[...])
        grad_rows = matmul(select[r], out_grad[...])
        for j in range(chunks):
            lanes = slice(j * LANES, (j + 1) * LANES)
            wide[r, pl.ds(j, experts, stride=units), :] = token_rows[:, lanes]
            wide[r, pl.ds(chunks + j, experts, stride=units), :] = row_weight * grad_rows[:, lanes]
        ready = wide[r].astype(BF).reshape(2, n, n, units, LANES)
        send0[r] = ready[0]
        send1[r] = ready[1]

    def first_stage(r):
        for i in offsets[:-1]:
            for p, (sent, mid, base) in enumerate(lines):
                other = turn(base, i)
                device = at(other, z, c) if p == 0 else at(y, other, c)
                remote(
                    sent.at[r, other], mid.at[r, base], s1_send.at[r, p], s1_recv.at[r, p], device
                ).start()
        for sent, mid, base in lines:
            mid[r, base] = sent[r, base]

    def first_copy(r, p):
        sent, mid, _ = lines[p]
        most = pl.ds(0, n - 1)
        return remote(
            sent.at[r, most], mid.at[r, most], s1_send.at[r, p], s1_recv.at[r, p], sibling
        )

    def second_stage(r):
        group = 2 * c + r
        for p, (sent, mid, slot) in enumerate(lines):
            base = z if p == 0 else y
            first_copy(r, p).wait_recv()
            for i in range(n):
                for j in range(n):
                    turned[r, p, i, j] = mid[r, j, i]
            for i in offsets[:-1]:
                other = turn(base, i)
                device = at(y, other, 0) if p == 0 else at(other, z, 1)
                remote(
                    turned.at[r, p, other], recv.at[group, base], s2_send, s2_recv.at[group], device
                ).start()

            @pl.when(c == p)
            def _():
                recv[group, base] = turned[r, p, base]

            @pl.when(c != p)
            def _():
                remote(
                    turned.at[r, p, base], recv.at[group, base], s2_send, s2_recv.at[group], sibling
                ).start()

    prepare(0)
    pl.semaphore_wait(barrier, len(greeted))

    first_stage(0)
    prepare(1)
    first_stage(1)
    for r in range(2):
        for p in range(2):
            first_copy(r, p).wait_send()

    second_stage(0)
    second_stage(1)

    triple, double = 3 * hidden_dim, 2 * hidden_dim
    first3, second3 = pl.ds(0, triple // 2), pl.ds(triple // 2, triple // 2)
    first2, second2 = pl.ds(0, hidden_dim), pl.ds(hidden_dim, hidden_dim)
    every = pl.ds(0, span)

    def hop(src, dst, sems, h, i, device):
        send_sem, recv_sem = sems
        return remote(src, dst, send_sem.at[h, i], recv_sem.at[h, i], {"dp": device})

    def sums(g, i):
        src, dst, device = (
            lambda: (psend.at[g, opposite, every, first3], prel.at[g, 0], right),
            lambda: (psend.at[g, opposite, every, second3], prel.at[g, 1], left),
            lambda: (psend.at[g, right, every, second3], precv.at[g, 0, every, second3], right),
            lambda: (psend.at[g, left, every, first3], precv.at[g, 1, every, first3], left),
            lambda: (psum.at[g, 0], precv.at[g, 0, every, first3], right),
            lambda: (psum.at[g, 1], precv.at[g, 1, every, second3], left),
        )[i]()
        return hop(src, dst, (p_send, p_recv), g, i, device)

    def gathers(g, i):
        owner, part, device = (
            (d, first2, right), (d, second2, left), (d, second2, right), (d, first2, left),
            (left, first2, right), (right, second2, left),
        )[i]
        piece = full.at[g, owner, every, part]
        return hop(piece, piece, (a_send, a_recv), g, i, device)

    def gathered(g, i):
        owner, part = (
            (left, first2), (right, second2), (left, second2), (right, first2),
            (opposite, first2), (opposite, second2),
        )[i]
        piece = full.at[g, owner, every, part]
        return hop(piece, piece, (a_send, a_recv), g, i, right)

    def hidden_copy(h, i):
        owner = lax.rem(d + PARTS - i, PARTS)
        send_piece, piece = hid.at[h, d], hid.at[h, owner]
        return (
            hop(send_piece, send_piece, (h_send, h_recv), h, i - 1, lax.rem(d + i, PARTS)),
            hop(piece, piece, (h_send, h_recv), h, i - 1, lax.rem(d + i, PARTS)),
        )

    def partial_sums(g):
        for same in range(2):
            count = n - 1 if same else n
            if count:
                part = recv.at[g, pl.ds(0, count)]

                @pl.when((c == g // 2) if same else (c != g // 2))
                def _():
                    remote(part, part, s2_send, s2_recv.at[g], sibling).wait_recv()

        came = block * units
        wide[g % 2, 0:came, :] = recv[g].reshape(came, LANES).astype(F32)
        rows = slice(g * block, (g + 1) * block)
        for j in range(chunks):
            lanes = slice(j * LANES, (j + 1) * LANES)
            for kind, target in enumerate((rows_all, grad_all)):
                target[rows, lanes] = wide[
                    g % 2, pl.ds(kind * chunks + j, block, stride=units), :
                ].astype(BF)
        if g == 0:
            for load in loads[5:]:
                load.wait()
        shape = (PARTS, span, hidden_dim)
        psend[g, :, :, 0:hidden_dim] = (
            matmul(rows_all[rows, :], gate[...]).astype(BF).reshape(shape)
        )
        psend[g, :, :, hidden_dim:double] = (
            matmul(rows_all[rows, :], up[...]).astype(BF).reshape(shape)
        )
        psend[g, :, :, double:] = (
            matmul(grad_all[rows, :], down[...], 1, 1).astype(BF).reshape(shape)
        )
        for i in range(4):
            sums(g, i).start()

    def pass_sums(g):
        middle = triple // 2
        sums(g, 0).wait_recv()
        psum[g, 0] = (
            psend[g, right, :, 0:middle].astype(F32) + prel[g, 0].astype(F32)
        ).astype(BF)
        sums(g, 4).start()
        sums(g, 1).wait_recv()
        psum[g, 1] = (
            psend[g, left, :, middle:].astype(F32) + prel[g, 1].astype(F32)
        ).astype(BF)
        sums(g, 5).start()

    def activations(g):
        for i in range(2, 6):
            sums(g, i).wait_recv()
        total = (
            psend[g, d].astype(F32) + precv[g, 0].astype(F32) + precv[g, 1].astype(F32)
        )
        gate_sum = total[:, 0:hidden_dim]
        up_sum = total[:, hidden_dim:double]
        hidden_grad = total[:, double:]
        sigma = jax.nn.sigmoid(gate_sum)
        active = gate_sum * sigma
        full[g, d, :, 0:hidden_dim] = (
            hidden_grad * up_sum * sigma * (1.0 + gate_sum * (1.0 - sigma))
        ).astype(BF)
        full[g, d, :, hidden_dim:] = (hidden_grad * active).astype(BF)
        for i in range(4):
            gathers(g, i).start()
        hid[g, d] = (active * up_sum).astype(BF)

    def pass_gathers(g):
        gathered(g, 0).wait_recv()
        gathers(g, 4).start()
        gathered(g, 1).wait_recv()
        gathers(g, 5).start()

    def row_gradients(h):
        for g in (2 * h, 2 * h + 1):
            for i in range(2, 6):
                gathered(g, i).wait_recv()
        back = full[2 * h : 2 * h + 2].reshape(experts, double)
        gate_back, up_back = back[:, 0:hidden_dim], back[:, hidden_dim:]
        row_back = matmul(gate_back, gate[...], 1, 1) + matmul(up_back, up[...], 1, 1)
        for r in range(2):
            for j in range(chunks):
                narrow[pl.ds(r * chunks + j, block, stride=units), :] = row_back[
                    r * block : (r + 1) * block, j * LANES : (j + 1) * LANES
                ]
        ret[h] = narrow[0 : block * units, :].astype(BF).reshape(n, n, units, LANES)

    def give_back(h):
        along, across = jnp.where(c == 0, z, y), jnp.where(c == 0, y, z)
        slots = [turn(along, i) for i in offsets]
        others = [turn(across, i) for i in offsets]
        to_slot = [slot * jnp.where(c == 0, 2, 2 * n) + h for slot in slots]
        to_other = [other * jnp.where(c == 0, 2 * n, 2) for other in others]
        for i, slot in enumerate(slots):
            for k, other in enumerate(others):
                copy = remote(
                    ret.at[h, slot, other], fin.at[c, across, along], r_send.at[h], r_recv,
                    {"expert": to_slot[i] + to_other[k]},
                )
                if offsets[i] or offsets[k]:
                    copy.start()
                else:
                    pl.when(c != h)(copy.start)

        @pl.when(c == h)
        def _():
            fin[c, across, along] = ret[h, along, across]

    partial_sums(0)
    partial_sums(2)
    partial_sums(1)
    partial_sums(3)
    pass_sums(0)
    pass_sums(2)
    pass_sums(1)
    pass_sums(3)
    activations(0)
    activations(2)
    activations(1)
    activations(3)
    pass_gathers(0)
    pass_gathers(2)
    pass_gathers(1)
    pass_gathers(3)
    row_gradients(0)
    give_back(0)
    row_gradients(1)
    give_back(1)
    for g in range(4):
        for i in range(1, PARTS):
            hidden_copy(g, i)[0].start()

    stores = []

    def store(i, src, dst):
        stores.append(pltpu.make_async_copy(src, dst, store_sem.at[i]))
        stores[-1].start()

    def weight_gradient(part, result, out):
        back = full[:, :, :, part * hidden_dim : (part + 1) * hidden_dim]
        back = back.reshape(2 * experts, hidden_dim)
        result[...] = matmul(rows_all[...], back, 0, 0).astype(BF)
        store(part, result, out.at[0])

    weight_gradient(0, gate_grad, gate_grad_hbm)
    weight_gradient(1, up_grad, up_grad_hbm)
    for g in range(4):
        for i in range(1, PARTS):
            hidden_copy(g, i)[1].wait()
    hidden = hid[...].reshape(2 * experts, hidden_dim)
    down_grad[...] = matmul(hidden, grad_all[...], 0, 0).astype(BF)
    store(2, down_grad, down_grad_hbm.at[0])

    for g in range(4):
        for i in range(6):
            sums(g, i).wait_send()
            gathers(g, i).wait_send()
    pieces = fin.reshape(experts, units, LANES)
    for same in range(2):
        count = block - 1 if same else block
        for h in range(2):
            if count:
                part = pieces.at[pl.ds(0, count)]

                @pl.when((c == h) if same else (c != h))
                def _():
                    remote(part, part, r_send.at[h], r_recv, sibling).wait_send()

    moved = recv.reshape(4 * n, n, units, LANES).at[pl.ds(0, 4 * n - 2)]
    remote(moved, moved, s2_send, s2_recv.at[0], sibling).wait_send()

    part = pieces.at[pl.ds(0, experts - 1)]
    remote(part, part, r_send.at[0], r_recv, sibling).wait_recv()
    narrow[...] = fin[...].reshape(experts * units, LANES).astype(F32)
    for j in range(chunks):
        total = jnp.zeros((count_tok, LANES), F32)
        for r in range(2):
            came = narrow[pl.ds(r * chunks + j, experts, stride=units), :].astype(BF)
            total = total + matmul(select[r], came, 0, 0)
        in_grad[:, j * LANES : (j + 1) * LANES] = total.astype(BF)
    store(3, in_grad, in_grad_hbm)
    for copy in stores:
        copy.wait()


def hand_over(*refs):
    count = (len(refs) - 2) // 3
    given, kept, passed = refs[:count], refs[count : 2 * count], refs[2 * count : 3 * count]
    come, go = refs[-2:]
    pieces = []
    for i in range(count):
        rows = given[i].shape[-2]
        step = max(rows // 4, min(rows, 32))
        for at in range(0, rows, step):
            part = (0, pl.ds(at, step)) if len(given[i].shape) == 3 else (pl.ds(at, step),)
            pieces.append((given[i].at[part], passed[i].at[part], kept[i].at[part]))
    reads = [pltpu.make_async_copy(src, mid, come.at[k]) for k, (src, mid, _) in enumerate(pieces)]
    writes = [pltpu.make_async_copy(mid, dst, go.at[k]) for k, (_, mid, dst) in enumerate(pieces)]
    for read in reads:
        read.start()
    for read, write in zip(reads, writes):
        read.wait()
        write.start()
    for write in writes:
        write.wait()


def local(tokens, out_grad, routes, route_weight, placement, gate_weight, up_weight, down_weight):
    experts = lax.axis_size("expert")
    side = 1
    while 2 * side * side < experts:
        side *= 2
    n = side
    count_tok, width = tokens.shape
    chosen = routes.shape[1]
    _, _, hidden_dim = gate_weight.shape
    units = 2 * width // LANES
    span = experts // (2 * PARTS)
    hbm = pl.BlockSpec(memory_space=pltpu.HBM)
    dma = pltpu.SemaphoreType.DMA

    def buf(*shape, dtype=BF):
        return pltpu.VMEM(shape, dtype)

    shapes = (
        jax.ShapeDtypeStruct((count_tok, width), BF),
        jax.ShapeDtypeStruct(gate_weight.shape, BF),
        jax.ShapeDtypeStruct(up_weight.shape, BF),
        jax.ShapeDtypeStruct(down_weight.shape, BF),
    )
    results = pl.pallas_call(
        functools.partial(kernel, side),
        out_shape=shapes,
        in_specs=[hbm] * 8,
        out_specs=(hbm,) * 4,
        scratch_shapes=[
            buf(count_tok, width), buf(count_tok, width),
            buf(chosen, count_tok, dtype=jnp.int32), buf(chosen, count_tok, dtype=F32),
            buf(1, experts, dtype=jnp.int32),
            buf(width, hidden_dim), buf(width, hidden_dim), buf(hidden_dim, width),
            buf(count_tok, width),
            buf(width, hidden_dim), buf(width, hidden_dim), buf(hidden_dim, width),
            buf(2, n, n, units, LANES), buf(2, n, n, units, LANES),
            buf(2, n, n, units, LANES), buf(2, n, n, units, LANES),
            buf(4, n, n, units, LANES),
            buf(2 * experts, width), buf(2 * experts, width),
            buf(2, 2, n, n, units, LANES),
            buf(4, PARTS, span, 3 * hidden_dim),
            buf(4, 2, span, 3 * hidden_dim // 2),
            buf(4, 2, span, 3 * hidden_dim // 2),
            buf(4, 2, span, 3 * hidden_dim),
            buf(4, PARTS, span, 2 * hidden_dim),
            buf(4, PARTS, span, hidden_dim),
            buf(2, n, n, units, LANES), buf(2, n, n, units, LANES),
            buf(2, experts * units, LANES, dtype=F32),
            buf(experts * units, LANES, dtype=F32),
            buf(2, experts, count_tok),
            dma((8,)), dma((4,)),
            dma((2, 2)), dma((2, 2)), dma, dma((4,)),
            dma((4, 6)), dma((4, 6)), dma((4, 6)), dma((4, 6)), dma((4, 3)), dma((4, 3)),
            dma((2,)), dma,
        ],
        compiler_params=pltpu.CompilerParams(
            collective_id=0, has_side_effects=True, vmem_limit_bytes=61 << 20
        ),
        name="expert_backward",
    )(
        tokens, out_grad, routes.T, route_weight.T, placement.reshape(1, experts),
        gate_weight, up_weight, down_weight,
    )
    return pl.pallas_call(
        hand_over,
        out_shape=shapes,
        in_specs=[hbm] * 4,
        out_specs=(hbm,) * 4,
        scratch_shapes=[buf(*shape.shape) for shape in shapes] + [dma((16,)), dma((16,))],
        compiler_params=pltpu.CompilerParams(vmem_limit_bytes=61 << 20),
        name="hand_over",
    )(*results)


def solution(mesh):
    in_specs = (
        P("expert", "dp"),
        P("expert", "dp"),
        P("expert", None),
        P("expert", None),
        P(),
        P("expert", "dp", None),
        P("expert", "dp", None),
        P("expert", None, "dp"),
    )
    out_specs = (
        P("expert", "dp"),
        P("expert", "dp", None),
        P("expert", "dp", None),
        P("expert", None, "dp"),
    )
    return jax.shard_map(local, mesh=mesh, in_specs=in_specs, out_specs=out_specs, check_vma=False)
```

```python
import functools

import jax
import jax.numpy as jnp
from jax import lax
from jax.experimental import pallas as pl
from jax.experimental.pallas import tpu as pltpu
from jax.sharding import PartitionSpec as P

BF = jnp.bfloat16
F32 = jnp.float32
LANES = 128
PARTS = 4


def matmul(left, right, left_dim=1, right_dim=0):
    return lax.dot_general(
        left, right, (((left_dim,), (right_dim,)), ((), ())), preferred_element_type=F32
    )


def remote(src, dst, send_sem, recv_sem, device):
    return pltpu.make_async_remote_copy(
        src_ref=src,
        dst_ref=dst,
        send_sem=send_sem,
        recv_sem=recv_sem,
        device_id=device,
        device_id_type=pl.DeviceIdType.MESH,
    )


def kernel(
    side,
    tokens_hbm, out_grad_hbm, routes_hbm, weight_hbm, placement_hbm, gate_hbm, up_hbm, down_hbm,
    in_grad_hbm, gate_grad_hbm, up_grad_hbm, down_grad_hbm,
    tokens, out_grad, routes, route_weight, placement, gate, up, down,
    in_grad, gate_grad, up_grad, down_grad,
    send0, send1, mid0, mid1, recv, rows_all, grad_all,
    turned, psend, psum, prel, precv, full, hid, ret, fin, wide, narrow, select,
    load_sem, store_sem, s1_send, s1_recv, s2_send, s2_recv,
    p_send, p_recv, a_send, a_recv, h_send, h_recv, r_send, r_recv,
):
    n = side
    block = n * n
    experts = 2 * block
    count_tok, width = tokens.shape
    chunks = width // LANES
    units = 2 * chunks
    hidden_dim = gate.shape[1]
    chosen = routes.shape[0]
    span = block // PARTS
    me = lax.axis_index("expert")
    d = lax.axis_index("dp")
    y = me // (2 * n)
    z = lax.rem(me // 2, n)
    c = lax.rem(me, 2)

    def at(yy, zz, cc):
        return {"expert": (yy * n + zz) * 2 + cc}

    def turn(base, i):
        return jnp.bitwise_and(base + i, n - 1)

    offsets = sorted(range(n), key=lambda i: (-min(i, n - i), i))

    sibling = at(y, z, 1 - c)

    loads = [
        pltpu.make_async_copy(src, dst, load_sem.at[i])
        for i, (src, dst) in enumerate(
            (
                (placement_hbm, placement), (routes_hbm, routes), (weight_hbm, route_weight),
                (tokens_hbm, tokens), (out_grad_hbm, out_grad),
                (gate_hbm.at[0], gate), (up_hbm.at[0], up), (down_hbm.at[0], down),
            )
        )
    ]
    for load in loads:
        load.start()

    barrier = pltpu.get_barrier_semaphore()
    greeted = [sibling]
    for i in range(1, n):
        for cc in range(2):
            greeted += [at(turn(y, i), z, cc), at(y, turn(z, i), cc)]
    right, left = lax.rem(d + 1, PARTS), lax.rem(d + PARTS - 1, PARTS)
    opposite = lax.rem(d + 2, PARTS)
    greeted += [{"dp": right}, {"dp": left}, {"dp": opposite}]
    for device in greeted:
        pl.semaphore_signal(
            barrier, inc=1, device_id=device, device_id_type=pl.DeviceIdType.MESH
        )
    for load in loads[:5]:
        load.wait()

    place = placement[...]
    place_y, place_z, place_c = place // (2 * n), lax.rem(place // 2, n), lax.rem(place, 2)
    spot = jnp.where(place_c == 0, place_y * n + place_z, block + place_z * n + place_y)
    spot = jnp.transpose(jnp.broadcast_to(spot.astype(F32), (LANES, experts)))[:, :count_tok]
    expert_ids = lax.broadcasted_iota(jnp.int32, (experts, count_tok), 0)
    expert_ids_f = expert_ids.astype(F32)
    named = jnp.zeros((experts, count_tok), F32)
    weight = jnp.zeros((experts, count_tok), F32)
    for k in range(chosen):
        hit = routes[k : k + 1, :] == expert_ids
        where = jnp.sum(jnp.where(hit, spot, 0.0), axis=0, keepdims=True)
        mine = where == expert_ids_f
        named = jnp.where(mine, 1.0, named)
        weight = jnp.where(mine, route_weight[k : k + 1, :], weight)
    before = (
        lax.broadcasted_iota(jnp.int32, (count_tok, count_tok), 0)
        < lax.broadcasted_iota(jnp.int32, (count_tok, count_tok), 1)
    ).astype(BF)
    rank = matmul(named.astype(BF), before)

    lines = ((send0, mid0, y), (send1, mid1, z))

    def prepare(r):
        chosen_rank = rank < 0.5 if r == 0 else rank > 0.5
        pick = jnp.where(chosen_rank, named, 0.0)
        select[r] = pick.astype(BF)
        row_weight = jnp.sum(pick * weight, axis=1, keepdims=True)
        token_rows = matmul(select[r], tokens[...])
        grad_rows = matmul(select[r], out_grad[...])
        for j in range(chunks):
            lanes = slice(j * LANES, (j + 1) * LANES)
            wide[r, pl.ds(j, experts, stride=units), :] = token_rows[:, lanes]
            wide[r, pl.ds(chunks + j, experts, stride=units), :] = row_weight * grad_rows[:, lanes]
        ready = wide[r].astype(BF).reshape(2, n, n, units, LANES)
        send0[r] = ready[0]
        send1[r] = ready[1]

    def first_stage(r):
        for i in offsets[:-1]:
            for p, (sent, mid, base) in enumerate(lines):
                other = turn(base, i)
                device = at(other, z, c) if p == 0 else at(y, other, c)
                remote(
                    sent.at[r, other], mid.at[r, base], s1_send.at[r, p], s1_recv.at[r, p], device
                ).start()
        for sent, mid, base in lines:
            mid[r, base] = sent[r, base]

    def first_copy(r, p):
        sent, mid, _ = lines[p]
        most = pl.ds(0, n - 1)
        return remote(
            sent.at[r, most], mid.at[r, most], s1_send.at[r, p], s1_recv.at[r, p], sibling
        )

    def second_stage(r):
        group = 2 * c + r
        for p, (sent, mid, slot) in enumerate(lines):
            base = z if p == 0 else y
            first_copy(r, p).wait_recv()
            for i in range(n):
                for j in range(n):
                    turned[r, p, i, j] = mid[r, j, i]
            for i in offsets[:-1]:
                other = turn(base, i)
                device = at(y, other, 0) if p == 0 else at(other, z, 1)
                remote(
                    turned.at[r, p, other], recv.at[group, base], s2_send, s2_recv.at[group], device
                ).start()

            @pl.when(c == p)
            def _():
                recv[group, base] = turned[r, p, base]

            @pl.when(c != p)
            def _():
                remote(
                    turned.at[r, p, base], recv.at[group, base], s2_send, s2_recv.at[group], sibling
                ).start()

    prepare(0)
    pl.semaphore_wait(barrier, len(greeted))

    first_stage(0)
    prepare(1)
    first_stage(1)
    second_stage(0)
    second_stage(1)

    triple, double = 3 * hidden_dim, 2 * hidden_dim
    first3, second3 = pl.ds(0, triple // 2), pl.ds(triple // 2, triple // 2)
    first2, second2 = pl.ds(0, hidden_dim), pl.ds(hidden_dim, hidden_dim)
    every = pl.ds(0, span)

    def hop(src, dst, sems, h, i, device):
        send_sem, recv_sem = sems
        return remote(src, dst, send_sem.at[h, i], recv_sem.at[h, i], {"dp": device})

    def sums(g, i):
        src, dst, device = (
            lambda: (psend.at[g, opposite, every, first3], prel.at[g, 0], right),
            lambda: (psend.at[g, opposite, every, second3], prel.at[g, 1], left),
            lambda: (psend.at[g, right, every, second3], precv.at[g, 0, every, second3], right),
            lambda: (psend.at[g, left, every, first3], precv.at[g, 1, every, first3], left),
            lambda: (psum.at[g, 0], precv.at[g, 0, every, first3], right),
            lambda: (psum.at[g, 1], precv.at[g, 1, every, second3], left),
        )[i]()
        return hop(src, dst, (p_send, p_recv), g, i, device)

    def gathers(g, i):
        owner, part, device = (
            (d, first2, right), (d, second2, left), (d, second2, right), (d, first2, left),
            (left, first2, right), (right, second2, left),
        )[i]
        piece = full.at[g, owner, every, part]
        return hop(piece, piece, (a_send, a_recv), g, i, device)

    def gathered(g, i):
        owner, part = (
            (left, first2), (right, second2), (left, second2), (right, first2),
            (opposite, first2), (opposite, second2),
        )[i]
        piece = full.at[g, owner, every, part]
        return hop(piece, piece, (a_send, a_recv), g, i, right)

    def hidden_copy(h, i):
        owner = lax.rem(d + PARTS - i, PARTS)
        send_piece, piece = hid.at[h, d], hid.at[h, owner]
        return (
            hop(send_piece, send_piece, (h_send, h_recv), h, i - 1, lax.rem(d + i, PARTS)),
            hop(piece, piece, (h_send, h_recv), h, i - 1, lax.rem(d + i, PARTS)),
        )

    def partial_sums(g):
        for same in range(2):
            count = n - 1 if same else n
            if count:
                part = recv.at[g, pl.ds(0, count)]

                @pl.when((c == g // 2) if same else (c != g // 2))
                def _():
                    remote(part, part, s2_send, s2_recv.at[g], sibling).wait_recv()

        came = block * units
        wide[g % 2, 0:came, :] = recv[g].reshape(came, LANES).astype(F32)
        rows = slice(g * block, (g + 1) * block)
        for j in range(chunks):
            lanes = slice(j * LANES, (j + 1) * LANES)
            for kind, target in enumerate((rows_all, grad_all)):
                target[rows, lanes] = wide[
                    g % 2, pl.ds(kind * chunks + j, block, stride=units), :
                ].astype(BF)
        if g == 0:
            for load in loads[5:]:
                load.wait()
        shape = (PARTS, span, hidden_dim)
        psend[g, :, :, 0:hidden_dim] = (
            matmul(rows_all[rows, :], gate[...]).astype(BF).reshape(shape)
        )
        psend[g, :, :, hidden_dim:double] = (
            matmul(rows_all[rows, :], up[...]).astype(BF).reshape(shape)
        )
        for i in (0, 3):
            sums(g, i).start()
        psend[g, :, :, double:] = (
            matmul(grad_all[rows, :], down[...], 1, 1).astype(BF).reshape(shape)
        )
        for i in (1, 2):
            sums(g, i).start()

    def pass_sums(g):
        middle = triple // 2
        sums(g, 0).wait_recv()
        psum[g, 0] = (
            psend[g, right, :, 0:middle].astype(F32) + prel[g, 0].astype(F32)
        ).astype(BF)
        sums(g, 4).start()
        sums(g, 1).wait_recv()
        psum[g, 1] = (
            psend[g, left, :, middle:].astype(F32) + prel[g, 1].astype(F32)
        ).astype(BF)
        sums(g, 5).start()

    def activations(g):
        for i in range(2, 6):
            sums(g, i).wait_recv()
        total = (
            psend[g, d].astype(F32) + precv[g, 0].astype(F32) + precv[g, 1].astype(F32)
        )
        gate_sum = total[:, 0:hidden_dim]
        up_sum = total[:, hidden_dim:double]
        hidden_grad = total[:, double:]
        sigma = jax.nn.sigmoid(gate_sum)
        active = gate_sum * sigma
        full[g, d, :, 0:hidden_dim] = (
            hidden_grad * up_sum * sigma * (1.0 + gate_sum * (1.0 - sigma))
        ).astype(BF)
        for i in (0, 3):
            gathers(g, i).start()
        full[g, d, :, hidden_dim:] = (hidden_grad * active).astype(BF)
        for i in (1, 2):
            gathers(g, i).start()
        hid[g, d] = (active * up_sum).astype(BF)

    def pass_gathers(g):
        gathered(g, 0).wait_recv()
        gathers(g, 4).start()
        gathered(g, 1).wait_recv()
        gathers(g, 5).start()

    def row_gradients(h):
        for g in (2 * h, 2 * h + 1):
            for i in range(2, 6):
                gathered(g, i).wait_recv()
        back = full[2 * h : 2 * h + 2].reshape(experts, double)
        gate_back, up_back = back[:, 0:hidden_dim], back[:, hidden_dim:]
        row_back = matmul(gate_back, gate[...], 1, 1) + matmul(up_back, up[...], 1, 1)
        for r in range(2):
            for j in range(chunks):
                narrow[pl.ds(r * chunks + j, block, stride=units), :] = row_back[
                    r * block : (r + 1) * block, j * LANES : (j + 1) * LANES
                ]
        ret[h] = narrow[0 : block * units, :].astype(BF).reshape(n, n, units, LANES)

    def give_back(h):
        along, across = jnp.where(c == 0, z, y), jnp.where(c == 0, y, z)
        slots = [turn(along, i) for i in offsets]
        others = [turn(across, i) for i in offsets]
        to_slot = [slot * jnp.where(c == 0, 2, 2 * n) + h for slot in slots]
        to_other = [other * jnp.where(c == 0, 2 * n, 2) for other in others]
        for i, slot in enumerate(slots):
            for k, other in enumerate(others):
                copy = remote(
                    ret.at[h, slot, other], fin.at[c, across, along], r_send.at[h], r_recv,
                    {"expert": to_slot[i] + to_other[k]},
                )
                if offsets[i] or offsets[k]:
                    copy.start()
                else:
                    pl.when(c != h)(copy.start)

        @pl.when(c == h)
        def _():
            fin[c, across, along] = ret[h, along, across]

    partial_sums(0)
    partial_sums(2)
    partial_sums(1)
    partial_sums(3)
    pass_sums(0)
    pass_sums(2)
    pass_sums(1)
    pass_sums(3)
    activations(0)
    activations(2)
    activations(1)
    activations(3)
    pass_gathers(0)
    pass_gathers(2)
    pass_gathers(1)
    pass_gathers(3)
    row_gradients(0)
    give_back(0)
    row_gradients(1)
    give_back(1)
    for g in range(4):
        for i in range(1, PARTS):
            hidden_copy(g, i)[0].start()

    stores = []

    def store(i, src, dst):
        stores.append(pltpu.make_async_copy(src, dst, store_sem.at[i]))
        stores[-1].start()

    def weight_gradient(part, result, out):
        back = full[:, :, :, part * hidden_dim : (part + 1) * hidden_dim]
        back = back.reshape(2 * experts, hidden_dim)
        result[...] = matmul(rows_all[...], back, 0, 0).astype(BF)
        store(part, result, out.at[0])

    weight_gradient(0, gate_grad, gate_grad_hbm)
    weight_gradient(1, up_grad, up_grad_hbm)
    for g in range(4):
        for i in range(1, PARTS):
            hidden_copy(g, i)[1].wait()
    hidden = hid[...].reshape(2 * experts, hidden_dim)
    down_grad[...] = matmul(hidden, grad_all[...], 0, 0).astype(BF)
    store(2, down_grad, down_grad_hbm.at[0])

    for g in range(4):
        for i in range(6):
            sums(g, i).wait_send()
            gathers(g, i).wait_send()
    pieces = fin.reshape(experts, units, LANES)
    for same in range(2):
        count = block - 1 if same else block
        for h in range(2):
            if count:
                part = pieces.at[pl.ds(0, count)]

                @pl.when((c == h) if same else (c != h))
                def _():
                    remote(part, part, r_send.at[h], r_recv, sibling).wait_send()

    for r in range(2):
        for p in range(2):
            first_copy(r, p).wait_send()
    moved = recv.reshape(4 * n, n, units, LANES).at[pl.ds(0, 4 * n - 2)]
    remote(moved, moved, s2_send, s2_recv.at[0], sibling).wait_send()

    part = pieces.at[pl.ds(0, experts - 1)]
    remote(part, part, r_send.at[0], r_recv, sibling).wait_recv()
    narrow[...] = fin[...].reshape(experts * units, LANES).astype(F32)
    for j in range(chunks):
        total = jnp.zeros((count_tok, LANES), F32)
        for r in range(2):
            came = narrow[pl.ds(r * chunks + j, experts, stride=units), :].astype(BF)
            total = total + matmul(select[r], came, 0, 0)
        in_grad[:, j * LANES : (j + 1) * LANES] = total.astype(BF)
    store(3, in_grad, in_grad_hbm)
    for copy in stores:
        copy.wait()


def hand_over(*refs):
    count = (len(refs) - 2) // 3
    given, kept, passed = refs[:count], refs[count : 2 * count], refs[2 * count : 3 * count]
    come, go = refs[-2:]
    pieces = []
    for i in range(count):
        rows = given[i].shape[-2]
        step = max(rows // 2, min(rows, 32))
        for at in range(0, rows, step):
            part = (0, pl.ds(at, step)) if len(given[i].shape) == 3 else (pl.ds(at, step),)
            pieces.append((given[i].at[part], passed[i].at[part], kept[i].at[part]))
    reads = [pltpu.make_async_copy(src, mid, come.at[k]) for k, (src, mid, _) in enumerate(pieces)]
    writes = [pltpu.make_async_copy(mid, dst, go.at[k]) for k, (_, mid, dst) in enumerate(pieces)]
    for read in reads:
        read.start()
    for read, write in zip(reads, writes):
        read.wait()
        write.start()
    for write in writes:
        write.wait()


def local(tokens, out_grad, routes, route_weight, placement, gate_weight, up_weight, down_weight):
    experts = lax.axis_size("expert")
    side = 1
    while 2 * side * side < experts:
        side *= 2
    n = side
    count_tok, width = tokens.shape
    chosen = routes.shape[1]
    _, _, hidden_dim = gate_weight.shape
    units = 2 * width // LANES
    span = experts // (2 * PARTS)
    hbm = pl.BlockSpec(memory_space=pltpu.HBM)
    dma = pltpu.SemaphoreType.DMA

    def buf(*shape, dtype=BF):
        return pltpu.VMEM(shape, dtype)

    shapes = (
        jax.ShapeDtypeStruct((count_tok, width), BF),
        jax.ShapeDtypeStruct(gate_weight.shape, BF),
        jax.ShapeDtypeStruct(up_weight.shape, BF),
        jax.ShapeDtypeStruct(down_weight.shape, BF),
    )
    results = pl.pallas_call(
        functools.partial(kernel, side),
        out_shape=shapes,
        in_specs=[hbm] * 8,
        out_specs=(hbm,) * 4,
        scratch_shapes=[
            buf(count_tok, width), buf(count_tok, width),
            buf(chosen, count_tok, dtype=jnp.int32), buf(chosen, count_tok, dtype=F32),
            buf(1, experts, dtype=jnp.int32),
            buf(width, hidden_dim), buf(width, hidden_dim), buf(hidden_dim, width),
            buf(count_tok, width),
            buf(width, hidden_dim), buf(width, hidden_dim), buf(hidden_dim, width),
            buf(2, n, n, units, LANES), buf(2, n, n, units, LANES),
            buf(2, n, n, units, LANES), buf(2, n, n, units, LANES),
            buf(4, n, n, units, LANES),
            buf(2 * experts, width), buf(2 * experts, width),
            buf(2, 2, n, n, units, LANES),
            buf(4, PARTS, span, 3 * hidden_dim),
            buf(4, 2, span, 3 * hidden_dim // 2),
            buf(4, 2, span, 3 * hidden_dim // 2),
            buf(4, 2, span, 3 * hidden_dim),
            buf(4, PARTS, span, 2 * hidden_dim),
            buf(4, PARTS, span, hidden_dim),
            buf(2, n, n, units, LANES), buf(2, n, n, units, LANES),
            buf(2, experts * units, LANES, dtype=F32),
            buf(experts * units, LANES, dtype=F32),
            buf(2, experts, count_tok),
            dma((8,)), dma((4,)),
            dma((2, 2)), dma((2, 2)), dma, dma((4,)),
            dma((4, 6)), dma((4, 6)), dma((4, 6)), dma((4, 6)), dma((4, 3)), dma((4, 3)),
            dma((2,)), dma,
        ],
        compiler_params=pltpu.CompilerParams(
            collective_id=0, has_side_effects=True, vmem_limit_bytes=61 << 20
        ),
        name="expert_backward",
    )(
        tokens, out_grad, routes.T, route_weight.T, placement.reshape(1, experts),
        gate_weight, up_weight, down_weight,
    )
    return pl.pallas_call(
        hand_over,
        out_shape=shapes,
        in_specs=[hbm] * 4,
        out_specs=(hbm,) * 4,
        scratch_shapes=[buf(*shape.shape) for shape in shapes] + [dma((16,)), dma((16,))],
        compiler_params=pltpu.CompilerParams(vmem_limit_bytes=61 << 20),
        name="hand_over",
    )(*results)


def solution(mesh):
    in_specs = (
        P("expert", "dp"),
        P("expert", "dp"),
        P("expert", None),
        P("expert", None),
        P(),
        P("expert", "dp", None),
        P("expert", "dp", None),
        P("expert", None, "dp"),
    )
    out_specs = (
        P("expert", "dp"),
        P("expert", "dp", None),
        P("expert", "dp", None),
        P("expert", None, "dp"),
    )
    return jax.shard_map(local, mesh=mesh, in_specs=in_specs, out_specs=out_specs, check_vma=False)
```
